128 devices in a mesh: sec: 32 (over z, y, x_hi), tpl: 4 (over x_lo, core).
Axes of the slice: x: 4 (x_hi: 2, x_lo: 2; x = x_hi * 2 + x_lo), y: 4, z: 4, core: 2. Of those that a mesh axis runs over, the one named last changes fastest.
Arguments:
- raw: float32 [24576, 899], P('sec'), may hold values from -6 to 6
- stencil: float32 [3, 5], replicated, may hold values from -1.5 to 1.5
- mad: float32 [24576], P('sec'), may hold values from 0.5 to 4
- templates: bfloat16 [2048, 512], P(('sec', 'tpl')), may hold values from -0.25 to 0.25
- shifts: int32 [2048, 32], P(None, 'sec'), may hold values from 0 to 256
- listed: int32 [32, 128], P('sec', 'tpl'), may hold values from 0 to 2047, as said below
- counts: int32 [32, 4], P('sec', 'tpl'), may hold values from 16 to 32, as said below
Outputs:
- stack: float32 [2048, 128], P(('sec', 'tpl'))
The draws below stay inside these ranges and needn't reach their ends.
Inputs may be any that keep to these rules, and one draw needn't show every extreme that they name: `listed`: each device's 32 entries (live or not) name templates of 32 different owners, template k being owned by device k // 16 along sec+tpl; so no two entries of one device's list lie in the same owner's rows. `counts`: one device has 32 live slots.
All inputs are finite; a program needn't handle non-finite values.
Results may differ from the reference program's by a relative error of at most 0.0034.
Values may be sent and summed in bfloat16 or wider, within the bound.
A program may use at most 64 MiB of HBM per device.

```python
import math
import jax
import jax.numpy as jnp
from jax import lax

CHAN_SEC = 768
LAGS = 128
MAX_SHIFT = 256
TLEN = 512
TPL_DEV = 16
SLOTS = 32
TEMPLATES = 2048
CHANNELS = 24576
LAG_EXT = 384
SAMPLES = 899
N_SEC = 32
N_TPL = 4


def draw_listed(key, part):
    key = jax.random.fold_in(key, 11)
    devices = N_SEC * N_TPL

    def one_device(subkey):
        first_key, second_key = jax.random.split(subkey, 2)
        owners = jax.random.permutation(first_key, devices)[:SLOTS]
        within = jax.random.randint(second_key, (SLOTS,), 0, TPL_DEV)
        return owners * TPL_DEV + within
    chosen = jax.vmap(one_device)(jax.random.split(key, devices))
    return chosen.reshape(N_SEC, N_TPL * SLOTS).astype(jnp.int32)


def draw_counts(key, part):
    key = jax.random.fold_in(key, 23)
    devices = N_SEC * N_TPL
    left_key, right_key, heavy_key = jax.random.split(key, 3)
    left = jax.random.randint(left_key, (devices,), 0, SLOTS)
    right = jax.random.randint(right_key, (devices,), 0, SLOTS)
    heavy = jax.random.randint(heavy_key, (), 0, devices)
    level = SLOTS // 2 + (left + right) // 4
    level = jnp.where(jnp.arange(devices) == heavy, SLOTS, level)
    return level.reshape(N_SEC, N_TPL).astype(jnp.int32)


def set_ends(drawn, own_key, least, largest):
    longest = drawn.shape.index(max(drawn.shape))
    spots = []
    for shift in (0, 1):
        where = [jax.random.randint(jax.random.fold_in(own_key, axis), (), 0, length) for axis, length in enumerate(drawn.shape)]
        where[longest] = (where[longest] + shift) % drawn.shape[longest]
        spots.append(tuple(where))
    return drawn.at[spots[0]].set(least).at[spots[1]].set(largest)


def levels(own_key, dims, pieces, least, top_value):
    gain = 1.0
    for axis_at, shards_of in pieces:
        steps = jax.random.uniform(jax.random.fold_in(jax.random.fold_in(own_key, 6), axis_at), (shards_of,), jnp.float32, least / len(pieces), top_value / len(pieces))
        gain = gain * jnp.repeat(jnp.exp(steps), dims[axis_at] // shards_of).reshape((-1,) + (1,) * (len(dims) - 1 - axis_at))
    return gain


def scatter_about(stream_key, extent, scale, reach, shards=(), kind=jnp.bfloat16):
    result = scale * jax.random.normal(stream_key, extent, jnp.float32)
    if shards:
        result = result * levels(stream_key, extent, shards, -0.22, 0.18)
    return jnp.clip(result, -reach, reach).astype(kind)


def setup_inputs(seed: int = 0) -> dict:
    key_of = jax.random.split(jax.random.key(seed), 8)
    raw = scatter_about(key_of[0], (CHANNELS, SAMPLES), 1.0, 6.0, ((0, 32),), jnp.float32)
    stencil = scatter_about(key_of[1], (3, 5), 0.3, 1.5, (), jnp.float32)
    mad = jnp.clip(jnp.exp(math.log(4.0) - 2.0794415 * jax.random.uniform(key_of[2], (CHANNELS,), jnp.float32) ** levels(key_of[2], (CHANNELS,), ((0, 32),), -0.2, 0.2)), 0.5, 4.0)
    templates = scatter_about(key_of[3], (TEMPLATES, TLEN), TLEN ** -0.5, 0.25, ((0, 128),))
    shifts = set_ends(jax.random.randint(key_of[4], (TEMPLATES, N_SEC), 0, MAX_SHIFT + 1), jax.random.fold_in(key_of[4], 1), 0, MAX_SHIFT).astype(jnp.int32)
    listed = draw_listed(jax.random.fold_in(key_of[7], 71), 0)
    counts = draw_counts(jax.random.fold_in(key_of[7], 71), 0)
    return {"raw": raw, "stencil": stencil, "mad": mad, "templates": templates, "shifts": shifts, "listed": listed, "counts": counts}


def robust(value):
    return value * lax.rsqrt(1.0 + value * value)

def banded(block):
    number = block.shape[0]
    period = TLEN + 128
    widened = jnp.concatenate([block, jnp.zeros((number, 128), block.dtype)], axis=1)
    repeated = jnp.tile(widened, (1, 128))[:, :128 * (period - 1)]
    return repeated.reshape(number, 128, period - 1)

def reference(raw, stencil, mad, templates, shifts, listed, counts):
    window = SAMPLES - 4
    padded = jnp.pad(raw, ((1, 1), (0, 0)))
    filtered = jnp.zeros((CHANNELS, window), jnp.float32)
    for across in range(3):
        for along in range(5):
            filtered = filtered + stencil[across, along] * padded[across:across + CHANNELS, along:along + window]
    rounded = lax.optimization_barrier((filtered / mad[:, None]).astype(jnp.bfloat16))
    whitened = rounded.astype(jnp.float32)
    lag_tiles = LAG_EXT // 128
    band_len = 128 + TLEN - 1
    slot_all = N_TPL * SLOTS
    per_section = whitened.reshape(N_SEC, CHAN_SEC, window)
    alive = (jnp.arange(SLOTS, dtype=jnp.int32)[None, None, :] < counts[:, :, None]).reshape(N_SEC, slot_all)
    wave_full = templates.astype(jnp.float32)

    def shifted(series, offset):
        return lax.dynamic_slice_in_dim(series, offset.astype(jnp.int32), LAGS)

    def section(inputs):
        data, names, column, living = inputs
        segments = jnp.stack([data[:, number * 128:number * 128 + band_len] for number in range(lag_tiles)])
        matrix = banded(wave_full[names])
        corr = jnp.einsum('mci,kti->mckt', segments, matrix, precision=lax.Precision.HIGHEST)
        summed = lax.optimization_barrier(jnp.sum(robust(corr), axis=1))
        lagged = jnp.transpose(summed, (1, 0, 2)).reshape(slot_all, LAG_EXT)
        offsets = column[names]
        partial_value = jax.vmap(shifted)(lagged, offsets)
        return jnp.where(living[:, None], partial_value, jnp.zeros_like(partial_value))
    partials = lax.map(section, (per_section, listed, shifts.T, alive))
    flat_names = listed.reshape(-1)
    total = jax.ops.segment_sum(partials.reshape(-1, LAGS), flat_names, num_segments=TEMPLATES)
    tally = jax.ops.segment_sum(alive.reshape(-1).astype(jnp.float32), flat_names, num_segments=TEMPLATES)
    return total / jnp.sqrt(jnp.maximum(tally, 1.0) * CHAN_SEC)[:, None]
```

```python
import functools

import jax
import jax.numpy as jnp
from jax import lax
from jax.experimental import pallas as pl
from jax.experimental.pallas import tpu as pltpu
from jax.sharding import PartitionSpec as P

MESH = pl.DeviceIdType.MESH
DEVICES = 128
CHAN = 768
LAGS = 128
TLEN = 512
SLOTS = 32
OWN = 16
WINDOW = 768
WIDTH = 896
PAIRS = SLOTS // 2 + 1
NT = (((1,), (1,)), ((), ()))
TN = (((0,), (0,)), ((), ()))


def hops(step):
    return sum((0, 1, 2, 1)[d] for d in step[:3]) + 0.1 * step[3]


STEPS = sorted(
    [
        (dz, dy, dx, dc)
        for dz in range(4)
        for dy in range(4)
        for dx in range(4)
        for dc in range(2)
        if (dz, dy, dx, dc) != (0, 0, 0, 0)
    ],
    key=hops,
    reverse=True,
)


def peers():
    sec = lax.axis_index("sec")
    tpl = lax.axis_index("tpl")
    z = sec // 8
    y = sec // 2 % 4
    x = sec % 2 * 2 + tpl // 2
    core = tpl % 2
    zs = [(z + d) % 4 * 8 for d in range(4)]
    ys = [(y + d) % 4 * 2 for d in range(4)]
    xs = [(x + d) % 4 for d in range(4)]
    his = [v // 2 for v in xs]
    los = [v % 2 * 2 for v in xs]
    cores = [(core + d) % 2 for d in range(2)]
    out = []
    for dz, dy, dx, dc in STEPS:
        s = zs[dz] + ys[dy] + his[dx]
        t = los[dx] + cores[dc]
        out.append((s, t))
    return sec, tpl, out


def robust(value):
    return value * lax.rsqrt(1.0 + value * value)


def build(rows, shift):
    flat = jnp.concatenate(
        [jnp.broadcast_to(rows[k : k + 1], (8, 128)) for k in range(4)]
        + [jnp.zeros((8, WINDOW - TLEN), jnp.float32)],
        axis=1,
    )
    base = pltpu.roll(flat, shift, 1)
    base = pltpu.roll(base, 0, 1, stride=1, stride_axis=0)
    both = jnp.concatenate([base, pltpu.roll(base, 8, 1)], axis=0).astype(jnp.bfloat16)
    return jnp.concatenate([pltpu.roll(both, 16 * g, 1) if g else both for g in range(8)], axis=0)


def kernel(
    raw_ref,
    stencil_ref,
    mad_ref,
    templates_ref,
    shifts_ref,
    listed_ref,
    counts_ref,
    total_ref,
    tally_ref,
    raw_v,
    cu,
    white,
    inv_mad,
    name_out,
    name_in,
    row_out,
    row_in,
    part_out,
    part_in,
    info_v,
    info_s,
    acc,
    even_v,
    odd_v,
    *rest,
):
    bands = rest[:16]
    raw_sem, info_sem, halo_send, halo_recv, name_sems, row_sems, part_sems = rest[16:]
    sec, tpl, others = peers()
    me = sec * 4 + tpl

    load = pltpu.make_async_copy(raw_ref, raw_v, raw_sem)
    load.start()
    barrier = pltpu.get_barrier_semaphore()
    for s, t in others:
        pl.semaphore_signal(barrier, inc=1, device_id=(s, t), device_id_type=MESH)

    def send_all(src, dst, sems):
        for s, t in others:
            pltpu.make_async_remote_copy(
                src_ref=src.at[s * 4 + t],
                dst_ref=dst.at[me],
                send_sem=sems.at[0],
                recv_sem=sems.at[1],
                device_id=(s, t),
                device_id_type=MESH,
            ).start()
        pltpu.make_async_copy(src.at[me], dst.at[me], sems.at[1]).start()

    def got_all(src, dst, sems):
        pltpu.make_async_copy(src, dst, sems.at[1]).wait()

    def sent_all(src, dst, sems):
        part = pl.ds(0, DEVICES - 1)
        pltpu.make_async_copy(src.at[part], dst.at[part], sems.at[0]).wait()

    lane = lax.broadcasted_iota(jnp.int32, (SLOTS, 128), 1)
    slot = lax.broadcasted_iota(jnp.int32, (SLOTS, 128), 0)
    name = jnp.zeros((SLOTS, 128), jnp.int32)
    rest_shift = jnp.zeros((SLOTS, 128), jnp.int32)
    place = jnp.zeros((SLOTS, 128), jnp.int32)
    early_slots = jnp.int32(0)
    for q in range(SLOTS):
        k = listed_ref[0, q]
        moved = shifts_ref[k]
        late = (moved >= 128).astype(jnp.int32)
        spot = early_slots + late * (2 * PAIRS - 1 - q)
        early_slots = early_slots + 1 - late
        name = jnp.where(slot == q, k, name)
        rest_shift = jnp.where(slot == q, moved - 128 * late, rest_shift)
        place = jnp.where(slot == q, spot, place)
    owner = name // OWN
    within = name - owner * OWN
    live = slot < counts_ref[0, 0]
    own_hot = (owner == lane).astype(jnp.bfloat16)
    asked = jnp.where(live, within + 1, 0).astype(jnp.bfloat16)
    name_out[:, 0, :] = lax.dot_general(own_hot, asked, TN, preferred_element_type=jnp.float32)
    hot = place == lane
    info_v[0:1, :] = jnp.sum(jnp.where(hot, rest_shift, 0), axis=0, keepdims=True)
    info_v[1:2, :] = jnp.sum(jnp.where(hot, owner, 0), axis=0, keepdims=True)
    info_v[2:8, :] = jnp.zeros((6, 128), jnp.int32)
    info = pltpu.make_async_copy(info_v, info_s, info_sem)
    info.start()
    even_hot = (place == 2 * lane).astype(jnp.bfloat16)
    odd_hot = (place == 2 * lane + 1).astype(jnp.bfloat16)
    even_v[...] = lax.dot_general(even_hot, own_hot, TN, preferred_element_type=jnp.float32)
    odd_v[...] = lax.dot_general(odd_hot, own_hot, TN, preferred_element_type=jnp.float32)
    inv_mad[...] = jnp.broadcast_to(1.0 / mad_ref[...], (128, CHAN)).T
    acc[...] = jnp.zeros_like(acc)

    load.wait()
    for k in range(7):
        cu[8 : 8 + CHAN, 128 * k : 128 * k + 128] = raw_v[128 * k : 128 * k + 128, :].T
    tail = jnp.concatenate([raw_v[896:899, :], jnp.zeros((125, CHAN), jnp.float32)], axis=0)
    cu[8 : 8 + CHAN, 896:1024] = tail.T

    pl.semaphore_wait(barrier, DEVICES - 1)
    send_all(name_out, name_in, name_sems)
    up = pltpu.make_async_remote_copy(
        src_ref=cu.at[pl.ds(CHAN, 8)],
        dst_ref=cu.at[pl.ds(0, 8)],
        send_sem=halo_send.at[0],
        recv_sem=halo_recv.at[0],
        device_id=((sec + 1) % 32, tpl),
        device_id_type=MESH,
    )
    down = pltpu.make_async_remote_copy(
        src_ref=cu.at[pl.ds(8, 8)],
        dst_ref=cu.at[pl.ds(CHAN + 8, 8)],
        send_sem=halo_send.at[1],
        recv_sem=halo_recv.at[1],
        device_id=((sec + 31) % 32, tpl),
        device_id_type=MESH,
    )
    up.start()
    down.start()

    got_all(name_out, name_in, name_sems)
    wanted = name_in[:, 0, :]
    lanes = lax.broadcasted_iota(jnp.int32, (DEVICES, 128), 1)
    into = jnp.where(wanted.astype(jnp.int32) == lanes + 1, 1.0, 0.0)
    chosen = jnp.dot(
        into[:, :OWN].astype(jnp.bfloat16), templates_ref[...], preferred_element_type=jnp.float32
    )
    for k in range(4):
        row_out[:, k, :] = chosen[:, 128 * k : 128 * k + 128]
    send_all(row_out, row_in, row_sems)
    ones = jnp.ones((DEVICES, 128), jnp.bfloat16)
    tally = lax.dot_general(into.astype(jnp.bfloat16), ones, TN, preferred_element_type=jnp.float32)
    tally_ref[...] = tally[:OWN]

    up.wait()
    down.wait()

    def whiten(i, carry):
        base = pl.multiple_of(i * 16, 16)
        block = cu[pl.ds(base, 32), :]
        rows = lax.broadcasted_iota(jnp.int32, (16, 1024), 0) + base
        above = jnp.where((rows == 0) & (sec == 0), 0.0, block[7:23])
        below = jnp.where((rows == CHAN - 1) & (sec == 31), 0.0, block[9:25])
        middle = block[8:24]
        total = None
        for b in range(5):
            term = (
                stencil_ref[0, b] * above + stencil_ref[1, b] * middle + stencil_ref[2, b] * below
            )
            if b:
                term = pltpu.roll(term, 1024 - b, 1)
            term = term[:, :WIDTH]
            total = term if total is None else total + term
        scale = inv_mad[pl.ds(base, 16), :]
        scale = jnp.concatenate([scale] * (WIDTH // 128), axis=1)
        done = (total * scale).astype(jnp.bfloat16)
        white[0, pl.ds(base, 16), :] = done[:, :WINDOW]
        white[1, pl.ds(base, 16), :] = done[:, 128:]
        return carry

    lax.fori_loop(0, CHAN // 16, whiten, 0)

    info.wait()
    got_all(row_out, row_in, row_sems)

    def prepare(j, band):
        for h in range(2):
            rows = row_in[info_s[1, 2 * j + h]]
            band[128 * h : 128 * h + 128, :] = build(rows, info_s[0, 2 * j + h])

    def correlate(j, band):
        half = (2 * j >= early_slots).astype(jnp.int32)
        corr = lax.dot_general(white[half], band[...], NT, preferred_element_type=jnp.float32)
        acc[j] = robust(corr).reshape(CHAN // 8, 8, 256).sum(axis=0)

    for u in range(8):
        prepare(u, bands[u])
    for u in range(PAIRS):
        if u + 8 < PAIRS:
            prepare(u + 8, bands[(u + 8) % 16])
        correlate(u, bands[u % 16])

    sums = jnp.sum(acc[...], axis=1)
    part_out[:, 0, :] = lax.dot_general(
        even_v[:24], sums[:, :128], TN, precision=lax.Precision.HIGHEST,
        preferred_element_type=jnp.float32,
    ) + lax.dot_general(
        odd_v[:24], sums[:, 128:], TN, precision=lax.Precision.HIGHEST,
        preferred_element_type=jnp.float32,
    )
    send_all(part_out, part_in, part_sems)
    sent_all(name_out, name_in, name_sems)
    sent_all(row_out, row_in, row_sems)
    got_all(part_out, part_in, part_sems)
    total = lax.dot_general(
        into, part_in[:, 0, :], TN, precision=lax.Precision.HIGHEST,
        preferred_element_type=jnp.float32,
    )
    total_ref[...] = total[:OWN]
    sent_all(part_out, part_in, part_sems)


def shards(raw, stencil, mad, templates, shifts, listed, counts):
    vmem = pl.BlockSpec(memory_space=pltpu.VMEM)
    smem = pl.BlockSpec(memory_space=pltpu.SMEM)
    f32 = jnp.float32
    dma = pltpu.SemaphoreType.DMA
    out = jax.ShapeDtypeStruct((OWN, LAGS), f32)
    total, tally = pl.pallas_call(
        kernel,
        out_shape=(out, out),
        in_specs=[pl.BlockSpec(memory_space=pl.ANY), smem, vmem, vmem, smem, smem, smem],
        out_specs=(vmem, vmem),
        scratch_shapes=[
            pltpu.VMEM((899, CHAN), f32),
            pltpu.VMEM((CHAN + 16, 1024), f32),
            pltpu.VMEM((2, CHAN, WINDOW), jnp.bfloat16),
            pltpu.VMEM((CHAN, 128), f32),
            pltpu.VMEM((DEVICES, 1, 128), f32),
            pltpu.VMEM((DEVICES, 1, 128), f32),
            pltpu.VMEM((DEVICES, 4, 128), f32),
            pltpu.VMEM((DEVICES, 4, 128), f32),
            pltpu.VMEM((DEVICES, 1, 128), f32),
            pltpu.VMEM((DEVICES, 1, 128), f32),
            pltpu.VMEM((8, 128), jnp.int32),
            pltpu.SMEM((8, 128), jnp.int32),
            pltpu.VMEM((24, 8, 256), f32),
            pltpu.VMEM((128, 128), f32),
            pltpu.VMEM((128, 128), f32),
        ]
        + [pltpu.VMEM((256, WINDOW), jnp.bfloat16)] * 16
        + [dma, dma, dma((2,)), dma((2,)), dma((2,)), dma((2,)), dma((2,))],
        compiler_params=pltpu.CompilerParams(
            collective_id=0, has_side_effects=True, vmem_limit_bytes=60 * 2**20
        ),
        name="match",
    )(
        raw.T,
        stencil,
        mad.reshape(1, CHAN),
        templates,
        shifts.reshape(-1),
        listed,
        counts,
    )
    return total / jnp.sqrt(jnp.maximum(tally, 1.0) * CHAN)


def solution(mesh):
    in_specs = (
        P("sec", None),
        P(),
        P("sec"),
        P(("sec", "tpl"), None),
        P(None, "sec"),
        P("sec", "tpl"),
        P("sec", "tpl"),
    )
    out_specs = P(("sec", "tpl"), None)
    return jax.shard_map(shards, mesh=mesh, in_specs=in_specs, out_specs=out_specs, check_vma=False)
```

```python
import functools

import jax
import jax.numpy as jnp
from jax import lax
from jax.experimental import pallas as pl
from jax.experimental.pallas import tpu as pltpu
from jax.sharding import PartitionSpec as P

MESH = pl.DeviceIdType.MESH
DEVICES = 128
CHAN = 768
LAGS = 128
TLEN = 512
SLOTS = 32
OWN = 16
WINDOW = 768
WIDTH = 896
PAIRS = SLOTS // 2 + 1
NBANDS = 16
LEAD = 8
ROWS = 16
UNROLL = 4
TILES = WIDTH // 128
CUTS = (4, 6)
NT = (((1,), (1,)), ((), ()))
TN = (((0,), (0,)), ((), ()))


def hops(step):
    return sum((0, 1, 2, 1)[d] for d in step[:3])


STEPS = sorted(
    [
        (dz, dy, dx, dc)
        for dz in range(4)
        for dy in range(4)
        for dx in range(4)
        for dc in range(2)
    ],
    key=lambda step: (hops(step), step),
    reverse=True,
)
BACK = [
    STEPS.index(((4 - dz) % 4, (4 - dy) % 4, (4 - dx) % 4, dc)) for dz, dy, dx, dc in STEPS
]
SELF = DEVICES - 1
MID = sum(hops(step) >= 3 for step in STEPS)
GROUPS = ((MID, DEVICES), (0, MID))


def peers():
    sec = lax.axis_index("sec")
    tpl = lax.axis_index("tpl")
    z = sec // 8
    y = sec // 2 % 4
    x = sec % 2 * 2 + tpl // 2
    core = tpl % 2
    zs = [(z + d) % 4 * 8 for d in range(4)]
    ys = [(y + d) % 4 * 2 for d in range(4)]
    xs = [(x + d) % 4 for d in range(4)]
    his = [v // 2 for v in xs]
    los = [v % 2 * 2 for v in xs]
    cores = [(core + d) % 2 for d in range(2)]
    out = []
    for dz, dy, dx, dc in STEPS:
        s = zs[dz] + ys[dy] + his[dx]
        t = los[dx] + cores[dc]
        out.append((s, t))
    return sec, tpl, out


def robust(value):
    return value * lax.rsqrt(1.0 + value * value)


def build(rows, shift):
    flat = jnp.concatenate(
        [jnp.broadcast_to(rows[k : k + 1], (8, 128)) for k in range(4)]
        + [jnp.zeros((8, WINDOW - TLEN), jnp.float32)],
        axis=1,
    )
    base = pltpu.roll(flat, shift, 1)
    base = pltpu.roll(base, 0, 1, stride=1, stride_axis=0)
    both = jnp.concatenate([base, pltpu.roll(base, 8, 1)], axis=0).astype(jnp.bfloat16)
    return jnp.concatenate([pltpu.roll(both, 16 * g, 1) if g else both for g in range(8)], axis=0)


def split3(value):
    high = value.astype(jnp.bfloat16)
    left = value - high.astype(jnp.float32)
    middle = left.astype(jnp.bfloat16)
    low = (left - middle.astype(jnp.float32)).astype(jnp.bfloat16)
    return [high, middle, low]


def kernel(
    raw_hbm,
    stencil_hbm,
    mad_hbm,
    templates_hbm,
    shifts_hbm,
    listed_hbm,
    counts_hbm,
    total_ref,
    tally_ref,
    raw_v,
    stencil_ref,
    mad_ref,
    templates_ref,
    shifts_ref,
    listed_ref,
    counts_ref,
    tile_v,
    edge_v,
    halo_out,
    halo_in,
    white,
    inv_mad,
    name_out,
    name_in,
    row_out,
    row_in,
    part_out,
    part_in,
    info_v,
    info_s,
    acc,
    pick_v,
    *rest,
):
    bands = rest[:NBANDS]
    load_sems, info_sem, halo_send, halo_recv, name_sems, row_sems, part_sems = rest[NBANDS:]
    sec, tpl, others = peers()

    barrier = pltpu.get_barrier_semaphore()
    loads = [
        pltpu.make_async_copy(src, dst, load_sems.at[k])
        for k, (src, dst) in enumerate(
            [
                (listed_hbm, listed_ref),
                (counts_hbm, counts_ref),
                (shifts_hbm, shifts_ref),
                (stencil_hbm, stencil_ref),
                (mad_hbm, mad_ref),
                (templates_hbm, templates_ref),
            ]
            + [(raw_hbm.at[:, pl.ds(128 * k, 128)], raw_v.at[k, pl.ds(0, 899)]) for k in range(CHAN // 128)]
        )
    ]
    for copy in loads[:3]:
        copy.start()
    for s, t in others[:SELF]:
        pl.semaphore_signal(barrier, inc=1, device_id=(s, t), device_id_type=MESH)
    for copy in loads[3:]:
        copy.start()

    def send(src, dst, i, to, send_sem, recv_sem):
        s, t = others[to]
        pltpu.make_async_remote_copy(
            src_ref=src.at[i],
            dst_ref=dst.at[i],
            send_sem=send_sem,
            recv_sem=recv_sem,
            device_id=(s, t),
            device_id_type=MESH,
        ).start()

    def keep(src, dst, recv_sem):
        pltpu.make_async_copy(src.at[SELF], dst.at[SELF], recv_sem).start()

    def got(src, dst, lo, hi, recv_sem):
        part = pl.ds(lo, hi - lo)
        pltpu.make_async_copy(src.at[part], dst.at[part], recv_sem).wait()

    loads[0].wait()
    loads[1].wait()
    loads[2].wait()
    lane = lax.broadcasted_iota(jnp.int32, (SLOTS, 128), 1)
    slot = lax.broadcasted_iota(jnp.int32, (SLOTS, 128), 0)
    lane_row = lax.broadcasted_iota(jnp.int32, (8, 128), 1)
    ids = jnp.zeros((8, 128), jnp.int32)
    for i, (s, t) in enumerate(others):
        ids = jnp.where(lane_row == i, s * 4 + t, ids)
    ids = jnp.concatenate([ids] * (SLOTS // 8), axis=0)
    name = jnp.zeros((SLOTS, 128), jnp.int32)
    rest_shift = jnp.zeros((SLOTS, 128), jnp.int32)
    place = jnp.zeros((SLOTS, 128), jnp.int32)
    early_slots = jnp.int32(0)
    for q in range(SLOTS):
        k = listed_ref[0, q]
        moved = shifts_ref[k]
        late = (moved >= 128).astype(jnp.int32)
        spot = early_slots + late * (2 * PAIRS - 1 - q)
        early_slots = early_slots + 1 - late
        name = jnp.where(slot == q, k, name)
        rest_shift = jnp.where(slot == q, moved - 128 * late, rest_shift)
        place = jnp.where(slot == q, spot, place)
    owner = name // OWN
    within = name - owner * OWN
    live = slot < counts_ref[0, 0]
    owned = owner == ids
    own_hot = owned.astype(jnp.bfloat16)
    asked = jnp.where(live, within + 1, 0).astype(jnp.bfloat16)
    name_out[:, 0, :] = lax.dot_general(own_hot, asked, TN, preferred_element_type=jnp.float32)

    pl.semaphore_wait(barrier, DEVICES - 1)
    for g in (1, 0):
        for i in range(*GROUPS[g]):
            if i < SELF:
                send(name_out, name_in, i, i, name_sems.at[3], name_sems.at[g])
    keep(name_out, name_in, name_sems.at[0])
    loads[5].wait()
    loads[3].wait()
    loads[4].wait()
    inv_mad[...] = jnp.broadcast_to((1.0 / mad_ref[...]).reshape(1, CHAN), (8, CHAN))
    for copy in loads[6:]:
        copy.wait()
    raw_v[:, 899:, :] = jnp.zeros((CHAN // 128, 5, 128), jnp.float32)
    chunks = CHAN // 128
    lane_block = lax.broadcasted_iota(jnp.int32, (ROWS, 128), 1)
    nothing = jnp.zeros((ROWS, 128), jnp.float32)

    def whiten_rows(start, base):
        across = [[], [], []]
        for k in range(chunks):
            taps = [raw_v[k, pl.ds(start + base + b, ROWS), :] for b in range(5)]
            for a in range(3):
                value = stencil_ref[a, 0] * taps[0]
                for b in range(1, 5):
                    value = value + stencil_ref[a, b] * taps[b]
                across[a].append(value)
        lower = [pltpu.roll(value, 1, 1) for value in across[0]]
        upper = [pltpu.roll(value, 127, 1) for value in across[2]]
        for k in range(chunks):
            left = jnp.where(lane_block == 0, lower[k - 1] if k else nothing, lower[k])
            right = jnp.where(
                lane_block == 127, upper[k + 1] if k < chunks - 1 else nothing, upper[k]
            )
            done = (across[1][k] + left + right) * inv_mad[0:1, 128 * k : 128 * k + 128]
            tile_v[pl.ds(base, ROWS), 128 * k : 128 * k + 128] = done

    def whiten(lo, hi):
        for t in range(lo, hi):

            def step(i, carry):
                for k in range(UNROLL):
                    whiten_rows(128 * t, pl.multiple_of((i * UNROLL + k) * ROWS, ROWS))
                return carry

            lax.fori_loop(0, 128 // ROWS // UNROLL, step, 0)
            here = slice(128 * t, 128 * t + 128)
            done = tile_v[:, :CHAN].T
            edge_v[0, :, here] = done[:16]
            edge_v[1, :, here] = done[CHAN - 16 :]
            done = done.astype(jnp.bfloat16)
            if t < TILES - 1:
                white[0, :, here] = done
            if t > 0:
                white[1, :, 128 * t - 128 : 128 * t] = done

    def halo(t):
        for side, k, a in ((0, chunks - 1, 0), (1, 0, 2)):
            value = stencil_ref[a, 0] * raw_v[k, 128 * t : 128 * t + 128, :]
            for b in range(1, 5):
                value = value + stencil_ref[a, b] * raw_v[k, 128 * t + b : 128 * t + b + 128, :]
            turned = value.T
            halo_out[side, :, 128 * t : 128 * t + 128] = turned[:8] if side else turned[120:]

    for t in range(TILES):
        halo(t)
    up = pltpu.make_async_remote_copy(
        src_ref=halo_out.at[0],
        dst_ref=halo_in.at[0],
        send_sem=halo_send.at[0],
        recv_sem=halo_recv.at[0],
        device_id=((sec + 1) % 32, tpl),
        device_id_type=MESH,
    )
    down = pltpu.make_async_remote_copy(
        src_ref=halo_out.at[1],
        dst_ref=halo_in.at[1],
        send_sem=halo_send.at[1],
        recv_sem=halo_recv.at[1],
        device_id=((sec + 31) % 32, tpl),
        device_id_type=MESH,
    )
    up.start()
    down.start()

    hot = place == lane
    index = jnp.sum(jnp.where(owned, lane, 0), axis=1, keepdims=True)
    info_v[0:1, :] = jnp.sum(jnp.where(hot, rest_shift, 0), axis=0, keepdims=True)
    info_v[1:2, :] = jnp.sum(jnp.where(hot, index, 0), axis=0, keepdims=True)
    info_v[2:8, :] = jnp.zeros((6, 128), jnp.int32)
    info = pltpu.make_async_copy(info_v, info_s, info_sem)
    info.start()
    even_hot = (place == 2 * lane).astype(jnp.bfloat16)
    odd_hot = (place == 2 * lane + 1).astype(jnp.bfloat16)
    even = lax.dot_general(even_hot, own_hot, TN, preferred_element_type=jnp.float32)[:32]
    odd = lax.dot_general(odd_hot, own_hot, TN, preferred_element_type=jnp.float32)[:32]
    pick_v[...] = jnp.concatenate([even] * 3 + [odd] * 3, axis=0).astype(jnp.bfloat16)
    acc[...] = jnp.zeros_like(acc)

    def answer(g):
        lo, hi = GROUPS[g]
        got(name_out, name_in, lo, hi, name_sems.at[g])
        wanted = name_in[lo:hi, 0, :]
        lanes = lax.broadcasted_iota(jnp.int32, (hi - lo, 128), 1)
        into = jnp.where(wanted == (lanes + 1).astype(jnp.float32), 1.0, 0.0).astype(jnp.bfloat16)
        chosen = jnp.dot(into[:, :OWN], templates_ref[...], preferred_element_type=jnp.float32)
        for k in range(4):
            row_out[lo:hi, k, :] = chosen[:, 128 * k : 128 * k + 128]
        for i in range(lo, hi):
            if i < SELF:
                send(row_out, row_in, i, BACK[i], row_sems.at[0], row_sems.at[1])
        if hi == DEVICES:
            keep(row_out, row_in, row_sems.at[1])

    whiten(0, CUTS[0])
    answer(0)
    whiten(CUTS[0], CUTS[1])
    answer(1)
    whiten(CUTS[1], TILES)

    lanes = lax.broadcasted_iota(jnp.int32, (DEVICES, 128), 1)
    into = jnp.where(name_in[:, 0, :] == (lanes + 1).astype(jnp.float32), 1.0, 0.0)
    into = into.astype(jnp.bfloat16)
    ones = jnp.ones((DEVICES, 128), jnp.bfloat16)
    tally = lax.dot_general(into, ones, TN, preferred_element_type=jnp.float32)
    tally_ref[...] = tally[:OWN]

    up.wait()
    down.wait()
    edge_row = lax.broadcasted_iota(jnp.int32, (16, WIDTH), 0)
    for side, row, end, channel, start in ((0, 7, 0, 0, 0), (1, 0, 31, CHAN - 1, CHAN - 16)):
        extra = halo_in[side, row : row + 1, :] * inv_mad[0:1, channel : channel + 1]
        hit = (edge_row == channel - start) & (sec != end)
        done = (edge_v[side] + jnp.where(hit, extra, 0.0)).astype(jnp.bfloat16)
        white[0, start : start + 16, :] = done[:, :WINDOW]
        white[1, start : start + 16, :] = done[:, 128:]

    info.wait()
    got(row_out, row_in, 0, DEVICES, row_sems.at[1])

    def prepare(j, band):
        for h in range(2):
            rows = row_in[info_s[1, 2 * j + h]]
            band[128 * h : 128 * h + 128, :] = build(rows, info_s[0, 2 * j + h])

    def correlate(j, band):
        half = (2 * j >= early_slots).astype(jnp.int32)
        corr = lax.dot_general(white[half], band[...], NT, preferred_element_type=jnp.float32)
        acc[j] = robust(corr).reshape(CHAN // 8, 8, 256).sum(axis=0)

    for u in range(LEAD):
        prepare(u, bands[u])
    for u in range(PAIRS):
        if u + LEAD < PAIRS:
            prepare(u + LEAD, bands[(u + LEAD) % NBANDS])
        correlate(u, bands[u % NBANDS])

    sums = jnp.sum(acc[...], axis=1)
    parts = jnp.concatenate(split3(sums[:, :128]) + split3(sums[:, 128:]), axis=0)
    part_out[:, 0, :] = lax.dot_general(pick_v[...], parts, TN, preferred_element_type=jnp.float32)
    for i in range(SELF):
        send(part_out, part_in, i, i, part_sems.at[0], part_sems.at[1])
    keep(part_out, part_in, part_sems.at[1])
    into = jnp.concatenate([into] * 3, axis=0)
    got(name_out, name_in, 0, SELF, name_sems.at[3])
    got(row_out, row_in, 0, SELF, row_sems.at[0])
    got(part_out, part_in, 0, DEVICES, part_sems.at[1])
    arrived = jnp.concatenate(split3(part_in[:, 0, :]), axis=0)
    total = lax.dot_general(into, arrived, TN, preferred_element_type=jnp.float32)
    total_ref[...] = total[:OWN]
    got(part_out, part_in, 0, SELF, part_sems.at[0])


def shards(raw, stencil, mad, templates, shifts, listed, counts):
    vmem = pl.BlockSpec(memory_space=pltpu.VMEM)
    hbm = pl.BlockSpec(memory_space=pl.ANY)
    f32 = jnp.float32
    dma = pltpu.SemaphoreType.DMA
    out = jax.ShapeDtypeStruct((OWN, LAGS), f32)
    total, tally = pl.pallas_call(
        kernel,
        out_shape=(out, out),
        in_specs=[hbm] * 7,
        out_specs=(vmem, vmem),
        scratch_shapes=[
            pltpu.VMEM((CHAN // 128, 904, 128), f32),
            pltpu.SMEM((3, 5), f32),
            pltpu.VMEM((CHAN,), f32),
            pltpu.VMEM((OWN, TLEN), jnp.bfloat16),
            pltpu.SMEM((2048,), jnp.int32),
            pltpu.SMEM((1, SLOTS), jnp.int32),
            pltpu.SMEM((1, 1), jnp.int32),
            pltpu.VMEM((128, CHAN), f32),
            pltpu.VMEM((2, 16, WIDTH), f32),
            pltpu.VMEM((2, 8, WIDTH), f32),
            pltpu.VMEM((2, 8, WIDTH), f32),
            pltpu.VMEM((2, CHAN, WINDOW), jnp.bfloat16),
            pltpu.VMEM((8, CHAN), f32),
            pltpu.VMEM((DEVICES, 1, 128), f32),
            pltpu.VMEM((DEVICES, 1, 128), f32),
            pltpu.VMEM((DEVICES, 4, 128), f32),
            pltpu.VMEM((DEVICES, 4, 128), f32),
            pltpu.VMEM((DEVICES, 1, 128), f32),
            pltpu.VMEM((DEVICES, 1, 128), f32),
            pltpu.VMEM((8, 128), jnp.int32),
            pltpu.SMEM((8, 128), jnp.int32),
            pltpu.VMEM((32, 8, 256), f32),
            pltpu.VMEM((6 * 32, 128), jnp.bfloat16),
        ]
        + [pltpu.VMEM((256, WINDOW), jnp.bfloat16)] * NBANDS
        + [dma((12,)), dma, dma((2,)), dma((2,)), dma((4,)), dma((2,)), dma((2,))],
        compiler_params=pltpu.CompilerParams(
            collective_id=0, has_side_effects=True, vmem_limit_bytes=60 * 2**20
        ),
        name="match",
    )(raw.T, stencil, mad, templates, shifts.reshape(-1), listed, counts)
    return total / jnp.sqrt(jnp.maximum(tally, 1.0) * CHAN)


def solution(mesh):
    in_specs = (
        P("sec", None),
        P(),
        P("sec"),
        P(("sec", "tpl"), None),
        P(None, "sec"),
        P("sec", "tpl"),
        P("sec", "tpl"),
    )
    out_specs = P(("sec", "tpl"), None)
    return jax.shard_map(shards, mesh=mesh, in_specs=in_specs, out_specs=out_specs, check_vma=False)
```

```python
import functools

import jax
import jax.numpy as jnp
from jax import lax
from jax.experimental import pallas as pl
from jax.experimental.pallas import tpu as pltpu
from jax.sharding import PartitionSpec as P

MESH = pl.DeviceIdType.MESH
DEVICES = 128
CHAN = 768
LAGS = 128
TLEN = 512
SLOTS = 32
OWN = 16
WINDOW = 768
WIDTH = 896
PAIRS = SLOTS // 2 + 1
NBANDS = 16
LEAD = 8
ROWS = 16
UNROLL = 4
TILES = WIDTH // 128
CUTS = (4,)
NT = (((1,), (1,)), ((), ()))
TN = (((0,), (0,)), ((), ()))


def hops(step):
    return sum((0, 1, 2, 1)[d] for d in step[:3])


STEPS = sorted(
    [
        (dz, dy, dx, dc)
        for dz in range(4)
        for dy in range(4)
        for dx in range(4)
        for dc in range(2)
    ],
    key=lambda step: (hops(step), step),
    reverse=True,
)
BACK = [
    STEPS.index(((4 - dz) % 4, (4 - dy) % 4, (4 - dx) % 4, dc)) for dz, dy, dx, dc in STEPS
]
SELF = DEVICES - 1
GROUPS = ((0, DEVICES),)


def peers():
    sec = lax.axis_index("sec")
    tpl = lax.axis_index("tpl")
    z = sec // 8
    y = sec // 2 % 4
    x = sec % 2 * 2 + tpl // 2
    core = tpl % 2
    zs = [(z + d) % 4 * 8 for d in range(4)]
    ys = [(y + d) % 4 * 2 for d in range(4)]
    xs = [(x + d) % 4 for d in range(4)]
    his = [v // 2 for v in xs]
    los = [v % 2 * 2 for v in xs]
    cores = [(core + d) % 2 for d in range(2)]
    out = []
    for dz, dy, dx, dc in STEPS:
        s = zs[dz] + ys[dy] + his[dx]
        t = los[dx] + cores[dc]
        out.append((s, t))
    return sec, tpl, out


def robust(value):
    return value * lax.rsqrt(1.0 + value * value)


def build(rows, shift):
    flat = jnp.concatenate(
        [jnp.broadcast_to(rows[k : k + 1], (8, 128)) for k in range(4)]
        + [jnp.zeros((8, WINDOW - TLEN), jnp.float32)],
        axis=1,
    )
    base = pltpu.roll(flat, shift, 1)
    base = pltpu.roll(base, 0, 1, stride=1, stride_axis=0)
    both = jnp.concatenate([base, pltpu.roll(base, 8, 1)], axis=0).astype(jnp.bfloat16)
    return jnp.concatenate([pltpu.roll(both, 16 * g, 1) if g else both for g in range(8)], axis=0)


def split3(value):
    high = value.astype(jnp.bfloat16)
    left = value - high.astype(jnp.float32)
    middle = left.astype(jnp.bfloat16)
    low = (left - middle.astype(jnp.float32)).astype(jnp.bfloat16)
    return [high, middle, low]


def kernel(
    raw_hbm,
    stencil_hbm,
    mad_hbm,
    templates_hbm,
    shifts_hbm,
    listed_hbm,
    counts_hbm,
    total_ref,
    tally_ref,
    raw_v,
    stencil_ref,
    mad_ref,
    templates_ref,
    shifts_ref,
    listed_ref,
    counts_ref,
    tile_v,
    edge_v,
    halo_out,
    halo_in,
    white,
    inv_mad,
    name_out,
    name_in,
    row_out,
    row_in,
    part_out,
    part_in,
    info_v,
    info_s,
    acc,
    pick_v,
    *rest,
):
    bands = rest[:NBANDS]
    load_sems, info_sem, halo_send, halo_recv, name_sems, row_sems, part_sems = rest[NBANDS:]
    sec, tpl, others = peers()

    barrier = pltpu.get_barrier_semaphore()
    loads = [
        pltpu.make_async_copy(src, dst, load_sems.at[k])
        for k, (src, dst) in enumerate(
            [
                (listed_hbm, listed_ref),
                (counts_hbm, counts_ref),
                (shifts_hbm, shifts_ref),
                (stencil_hbm, stencil_ref),
                (mad_hbm, mad_ref),
                (templates_hbm, templates_ref),
            ]
            + [(raw_hbm.at[:, pl.ds(128 * k, 128)], raw_v.at[k, pl.ds(0, 899)]) for k in range(CHAN // 128)]
        )
    ]
    for copy in loads[:3]:
        copy.start()
    for s, t in others[:SELF]:
        pl.semaphore_signal(barrier, inc=1, device_id=(s, t), device_id_type=MESH)
    for copy in loads[3:]:
        copy.start()

    def send(src, dst, i, to, send_sem, recv_sem):
        s, t = others[to]
        pltpu.make_async_remote_copy(
            src_ref=src.at[i],
            dst_ref=dst.at[i],
            send_sem=send_sem,
            recv_sem=recv_sem,
            device_id=(s, t),
            device_id_type=MESH,
        ).start()

    def keep(src, dst, recv_sem):
        pltpu.make_async_copy(src.at[SELF], dst.at[SELF], recv_sem).start()

    def got(src, dst, lo, hi, recv_sem):
        part = pl.ds(lo, hi - lo)
        pltpu.make_async_copy(src.at[part], dst.at[part], recv_sem).wait()

    loads[0].wait()
    loads[1].wait()
    loads[2].wait()
    lane = lax.broadcasted_iota(jnp.int32, (SLOTS, 128), 1)
    slot = lax.broadcasted_iota(jnp.int32, (SLOTS, 128), 0)
    lane_row = lax.broadcasted_iota(jnp.int32, (8, 128), 1)
    ids = jnp.zeros((8, 128), jnp.int32)
    for i, (s, t) in enumerate(others):
        ids = jnp.where(lane_row == i, s * 4 + t, ids)
    ids = jnp.concatenate([ids] * (SLOTS // 8), axis=0)
    name = jnp.zeros((SLOTS, 128), jnp.int32)
    rest_shift = jnp.zeros((SLOTS, 128), jnp.int32)
    place = jnp.zeros((SLOTS, 128), jnp.int32)
    early_slots = jnp.int32(0)
    for q in range(SLOTS):
        k = listed_ref[0, q]
        moved = shifts_ref[k]
        late = (moved >= 128).astype(jnp.int32)
        spot = early_slots + late * (2 * PAIRS - 1 - q)
        early_slots = early_slots + 1 - late
        name = jnp.where(slot == q, k, name)
        rest_shift = jnp.where(slot == q, moved - 128 * late, rest_shift)
        place = jnp.where(slot == q, spot, place)
    owner = name // OWN
    within = name - owner * OWN
    live = slot < counts_ref[0, 0]
    owned = owner == ids
    own_hot = owned.astype(jnp.bfloat16)
    asked = jnp.where(live, within + 1, 0).astype(jnp.bfloat16)
    name_out[:, 0, :] = lax.dot_general(own_hot, asked, TN, preferred_element_type=jnp.float32)

    pl.semaphore_wait(barrier, DEVICES - 1)
    for g in (0,):
        for i in range(*GROUPS[g]):
            if i < SELF:
                send(name_out, name_in, i, i, name_sems.at[3], name_sems.at[g])
    keep(name_out, name_in, name_sems.at[0])
    loads[5].wait()
    loads[3].wait()
    loads[4].wait()
    inv_mad[...] = jnp.broadcast_to((1.0 / mad_ref[...]).reshape(1, CHAN), (8, CHAN))
    for copy in loads[6:]:
        copy.wait()
    raw_v[:, 899:, :] = jnp.zeros((CHAN // 128, 5, 128), jnp.float32)
    chunks = CHAN // 128
    lane_block = lax.broadcasted_iota(jnp.int32, (ROWS, 128), 1)
    nothing = jnp.zeros((ROWS, 128), jnp.float32)

    def whiten_rows(start, base):
        across = [[], [], []]
        for k in range(chunks):
            taps = [raw_v[k, pl.ds(start + base + b, ROWS), :] for b in range(5)]
            for a in range(3):
                value = stencil_ref[a, 0] * taps[0]
                for b in range(1, 5):
                    value = value + stencil_ref[a, b] * taps[b]
                across[a].append(value)
        lower = [pltpu.roll(value, 1, 1) for value in across[0]]
        upper = [pltpu.roll(value, 127, 1) for value in across[2]]
        for k in range(chunks):
            left = jnp.where(lane_block == 0, lower[k - 1] if k else nothing, lower[k])
            right = jnp.where(
                lane_block == 127, upper[k + 1] if k < chunks - 1 else nothing, upper[k]
            )
            done = (across[1][k] + left + right) * inv_mad[0:1, 128 * k : 128 * k + 128]
            tile_v[pl.ds(base, ROWS), 128 * k : 128 * k + 128] = done

    def whiten(lo, hi):
        for t in range(lo, hi):

            def step(i, carry):
                for k in range(UNROLL):
                    whiten_rows(128 * t, pl.multiple_of((i * UNROLL + k) * ROWS, ROWS))
                return carry

            lax.fori_loop(0, 128 // ROWS // UNROLL, step, 0)
            here = slice(128 * t, 128 * t + 128)
            done = tile_v[:, :CHAN].T
            edge_v[0, :, here] = done[:16]
            edge_v[1, :, here] = done[CHAN - 16 :]
            done = done.astype(jnp.bfloat16)
            if t < TILES - 1:
                white[0, :, here] = done
            if t > 0:
                white[1, :, 128 * t - 128 : 128 * t] = done

    def halo(t):
        for side, k, a in ((0, chunks - 1, 0), (1, 0, 2)):
            value = stencil_ref[a, 0] * raw_v[k, 128 * t : 128 * t + 128, :]
            for b in range(1, 5):
                value = value + stencil_ref[a, b] * raw_v[k, 128 * t + b : 128 * t + b + 128, :]
            turned = value.T
            halo_out[side, :, 128 * t : 128 * t + 128] = turned[:8] if side else turned[120:]

    for t in range(TILES):
        halo(t)
    up = pltpu.make_async_remote_copy(
        src_ref=halo_out.at[0],
        dst_ref=halo_in.at[0],
        send_sem=halo_send.at[0],
        recv_sem=halo_recv.at[0],
        device_id=((sec + 1) % 32, tpl),
        device_id_type=MESH,
    )
    down = pltpu.make_async_remote_copy(
        src_ref=halo_out.at[1],
        dst_ref=halo_in.at[1],
        send_sem=halo_send.at[1],
        recv_sem=halo_recv.at[1],
        device_id=((sec + 31) % 32, tpl),
        device_id_type=MESH,
    )
    up.start()
    down.start()

    hot = place == lane
    index = jnp.sum(jnp.where(owned, lane, 0), axis=1, keepdims=True)
    info_v[0:1, :] = jnp.sum(jnp.where(hot, rest_shift, 0), axis=0, keepdims=True)
    info_v[1:2, :] = jnp.sum(jnp.where(hot, index, 0), axis=0, keepdims=True)
    info_v[2:8, :] = jnp.zeros((6, 128), jnp.int32)
    info = pltpu.make_async_copy(info_v, info_s, info_sem)
    info.start()
    even_hot = (place == 2 * lane).astype(jnp.bfloat16)
    odd_hot = (place == 2 * lane + 1).astype(jnp.bfloat16)
    even = lax.dot_general(even_hot, own_hot, TN, preferred_element_type=jnp.float32)[:32]
    odd = lax.dot_general(odd_hot, own_hot, TN, preferred_element_type=jnp.float32)[:32]
    pick_v[...] = jnp.concatenate([even] * 3 + [odd] * 3, axis=0).astype(jnp.bfloat16)
    acc[...] = jnp.zeros_like(acc)

    def answer(g):
        lo, hi = GROUPS[g]
        got(name_out, name_in, lo, hi, name_sems.at[g])
        wanted = name_in[lo:hi, 0, :]
        lanes = lax.broadcasted_iota(jnp.int32, (hi - lo, 128), 1)
        into = jnp.where(wanted == (lanes + 1).astype(jnp.float32), 1.0, 0.0).astype(jnp.bfloat16)
        chosen = jnp.dot(into[:, :OWN], templates_ref[...], preferred_element_type=jnp.float32)
        row_out[lo:hi] = chosen.reshape(hi - lo, 4, 128).astype(jnp.bfloat16)
        for i in range(lo, hi):
            if i < SELF:
                send(row_out, row_in, i, BACK[i], row_sems.at[0], row_sems.at[1])
        if hi == DEVICES:
            keep(row_out, row_in, row_sems.at[1])

    whiten(0, CUTS[0])
    answer(0)
    whiten(CUTS[0], TILES)

    lanes = lax.broadcasted_iota(jnp.int32, (DEVICES, 128), 1)
    into = jnp.where(name_in[:, 0, :] == (lanes + 1).astype(jnp.float32), 1.0, 0.0)
    into = into.astype(jnp.bfloat16)
    ones = jnp.ones((DEVICES, 128), jnp.bfloat16)
    tally = lax.dot_general(into, ones, TN, preferred_element_type=jnp.float32)
    tally_ref[...] = tally[:OWN]

    up.wait()
    down.wait()
    edge_row = lax.broadcasted_iota(jnp.int32, (16, WIDTH), 0)
    for side, row, end, channel, start in ((0, 7, 0, 0, 0), (1, 0, 31, CHAN - 1, CHAN - 16)):
        extra = halo_in[side, row : row + 1, :] * inv_mad[0:1, channel : channel + 1]
        hit = (edge_row == channel - start) & (sec != end)
        done = (edge_v[side] + jnp.where(hit, extra, 0.0)).astype(jnp.bfloat16)
        white[0, start : start + 16, :] = done[:, :WINDOW]
        white[1, start : start + 16, :] = done[:, 128:]

    info.wait()
    got(row_out, row_in, 0, DEVICES, row_sems.at[1])

    def prepare(j, band):
        for h in range(2):
            rows = row_in[info_s[1, 2 * j + h]].astype(jnp.float32)
            band[128 * h : 128 * h + 128, :] = build(rows, info_s[0, 2 * j + h])

    def correlate(j, band):
        half = (2 * j >= early_slots).astype(jnp.int32)
        corr = lax.dot_general(white[half], band[...], NT, preferred_element_type=jnp.float32)
        acc[j] = robust(corr).reshape(CHAN // 8, 8, 256).sum(axis=0)

    for u in range(LEAD):
        prepare(u, bands[u])
    for u in range(PAIRS):
        if u + LEAD < PAIRS:
            prepare(u + LEAD, bands[(u + LEAD) % NBANDS])
        correlate(u, bands[u % NBANDS])

    sums = jnp.sum(acc[...], axis=1)
    parts = jnp.concatenate(split3(sums[:, :128]) + split3(sums[:, 128:]), axis=0)
    part_out[:, 0, :] = lax.dot_general(pick_v[...], parts, TN, preferred_element_type=jnp.float32)
    for i in range(SELF):
        send(part_out, part_in, i, i, part_sems.at[0], part_sems.at[1])
    keep(part_out, part_in, part_sems.at[1])
    into = jnp.concatenate([into] * 3, axis=0)
    got(name_out, name_in, 0, SELF, name_sems.at[3])
    got(row_out, row_in, 0, SELF, row_sems.at[0])
    got(part_out, part_in, 0, DEVICES, part_sems.at[1])
    arrived = jnp.concatenate(split3(part_in[:, 0, :]), axis=0)
    total = lax.dot_general(into, arrived, TN, preferred_element_type=jnp.float32)
    total_ref[...] = total[:OWN]
    got(part_out, part_in, 0, SELF, part_sems.at[0])


def shards(raw, stencil, mad, templates, shifts, listed, counts):
    vmem = pl.BlockSpec(memory_space=pltpu.VMEM)
    hbm = pl.BlockSpec(memory_space=pl.ANY)
    f32 = jnp.float32
    dma = pltpu.SemaphoreType.DMA
    out = jax.ShapeDtypeStruct((OWN, LAGS), f32)
    total, tally = pl.pallas_call(
        kernel,
        out_shape=(out, out),
        in_specs=[hbm] * 7,
        out_specs=(vmem, vmem),
        scratch_shapes=[
            pltpu.VMEM((CHAN // 128, 904, 128), f32),
            pltpu.SMEM((3, 5), f32),
            pltpu.VMEM((CHAN,), f32),
            pltpu.VMEM((OWN, TLEN), jnp.bfloat16),
            pltpu.SMEM((2048,), jnp.int32),
            pltpu.SMEM((1, SLOTS), jnp.int32),
            pltpu.SMEM((1, 1), jnp.int32),
            pltpu.VMEM((128, CHAN), f32),
            pltpu.VMEM((2, 16, WIDTH), f32),
            pltpu.VMEM((2, 8, WIDTH), f32),
            pltpu.VMEM((2, 8, WIDTH), f32),
            pltpu.VMEM((2, CHAN, WINDOW), jnp.bfloat16),
            pltpu.VMEM((8, CHAN), f32),
            pltpu.VMEM((DEVICES, 1, 128), f32),
            pltpu.VMEM((DEVICES, 1, 128), f32),
            pltpu.VMEM((DEVICES, 4, 128), jnp.bfloat16),
            pltpu.VMEM((DEVICES, 4, 128), jnp.bfloat16),
            pltpu.VMEM((DEVICES, 1, 128), f32),
            pltpu.VMEM((DEVICES, 1, 128), f32),
            pltpu.VMEM((8, 128), jnp.int32),
            pltpu.SMEM((8, 128), jnp.int32),
            pltpu.VMEM((32, 8, 256), f32),
            pltpu.VMEM((6 * 32, 128), jnp.bfloat16),
        ]
        + [pltpu.VMEM((256, WINDOW), jnp.bfloat16)] * NBANDS
        + [dma((12,)), dma, dma((2,)), dma((2,)), dma((4,)), dma((2,)), dma((2,))],
        compiler_params=pltpu.CompilerParams(
            collective_id=0, has_side_effects=True, vmem_limit_bytes=60 * 2**20
        ),
        name="match",
    )(raw.T, stencil, mad, templates, shifts.reshape(-1), listed, counts)
    return total / jnp.sqrt(jnp.maximum(tally, 1.0) * CHAN)


def solution(mesh):
    in_specs = (
        P("sec", None),
        P(),
        P("sec"),
        P(("sec", "tpl"), None),
        P(None, "sec"),
        P("sec", "tpl"),
        P("sec", "tpl"),
    )
    out_specs = P(("sec", "tpl"), None)
    return jax.shard_map(shards, mesh=mesh, in_specs=in_specs, out_specs=out_specs, check_vma=False)
```

```python
import functools

import jax
import jax.numpy as jnp
from jax import lax
from jax.experimental import pallas as pl
from jax.experimental.pallas import tpu as pltpu
from jax.sharding import PartitionSpec as P

MESH = pl.DeviceIdType.MESH
DEVICES = 128
CHAN = 768
LAGS = 128
TLEN = 512
SLOTS = 32
OWN = 16
WINDOW = 768
WIDTH = 896
PAIRS = SLOTS // 2 + 1
NBANDS = 16
LEAD = 8
ROWS = 16
UNROLL = 4
TILES = WIDTH // 128
CUTS = (4,)
NT = (((1,), (1,)), ((), ()))
TN = (((0,), (0,)), ((), ()))


def hops(step):
    return sum((0, 1, 2, 1)[d] for d in step[:3])


STEPS = sorted(
    [
        (dz, dy, dx, dc)
        for dz in range(4)
        for dy in range(4)
        for dx in range(4)
        for dc in range(2)
    ],
    key=lambda step: (hops(step), step),
    reverse=True,
)
BACK = [
    STEPS.index(((4 - dz) % 4, (4 - dy) % 4, (4 - dx) % 4, dc)) for dz, dy, dx, dc in STEPS
]
SELF = DEVICES - 1
GROUPS = ((0, DEVICES),)


def peers():
    sec = lax.axis_index("sec")
    tpl = lax.axis_index("tpl")
    z = sec // 8
    y = sec // 2 % 4
    x = sec % 2 * 2 + tpl // 2
    core = tpl % 2
    zs = [(z + d) % 4 * 8 for d in range(4)]
    ys = [(y + d) % 4 * 2 for d in range(4)]
    xs = [(x + d) % 4 for d in range(4)]
    his = [v // 2 for v in xs]
    los = [v % 2 * 2 for v in xs]
    cores = [(core + d) % 2 for d in range(2)]
    out = []
    for dz, dy, dx, dc in STEPS:
        s = zs[dz] + ys[dy] + his[dx]
        t = los[dx] + cores[dc]
        out.append((s, t))
    return sec, tpl, out


def robust(value):
    return value * lax.rsqrt(1.0 + value * value)


def build(rows, shift):
    flat = jnp.concatenate(
        [jnp.broadcast_to(rows[k : k + 1], (8, 128)) for k in range(4)]
        + [jnp.zeros((8, WINDOW - TLEN), jnp.float32)],
        axis=1,
    )
    base = pltpu.roll(flat, shift, 1)
    base = pltpu.roll(base, 0, 1, stride=1, stride_axis=0)
    return jnp.concatenate(
        [pltpu.roll(base, 8 * g, 1) if g else base for g in range(16)], axis=0
    ).astype(jnp.bfloat16)


def split3(value):
    high = value.astype(jnp.bfloat16)
    left = value - high.astype(jnp.float32)
    middle = left.astype(jnp.bfloat16)
    low = (left - middle.astype(jnp.float32)).astype(jnp.bfloat16)
    return [high, middle, low]


def kernel(
    raw_hbm,
    stencil_hbm,
    mad_hbm,
    templates_hbm,
    shifts_hbm,
    listed_hbm,
    counts_hbm,
    total_ref,
    tally_ref,
    raw_v,
    stencil_ref,
    mad_ref,
    templates_ref,
    shifts_ref,
    listed_ref,
    counts_ref,
    tile_v,
    edge_v,
    halo_out,
    halo_in,
    white,
    inv_mad,
    name_out,
    name_in,
    row_out,
    row_in,
    part_out,
    part_in,
    info_v,
    info_s,
    acc,
    pick_v,
    *rest,
):
    bands = rest[:NBANDS]
    load_sems, info_sem, halo_send, halo_recv, name_sems, row_sems, part_sems = rest[NBANDS:]
    sec, tpl, others = peers()

    barrier = pltpu.get_barrier_semaphore()
    loads = [
        pltpu.make_async_copy(src, dst, load_sems.at[k])
        for k, (src, dst) in enumerate(
            [
                (listed_hbm, listed_ref),
                (counts_hbm, counts_ref),
                (shifts_hbm, shifts_ref),
                (stencil_hbm, stencil_ref),
                (mad_hbm, mad_ref),
                (templates_hbm, templates_ref),
            ]
            + [(raw_hbm.at[:, pl.ds(128 * k, 128)], raw_v.at[k, pl.ds(0, 899)]) for k in range(CHAN // 128)]
        )
    ]
    for copy in loads[:3]:
        copy.start()
    for s, t in others[:SELF]:
        pl.semaphore_signal(barrier, inc=1, device_id=(s, t), device_id_type=MESH)
    for copy in loads[3:]:
        copy.start()

    def send(src, dst, i, to, send_sem, recv_sem):
        s, t = others[to]
        pltpu.make_async_remote_copy(
            src_ref=src.at[i],
            dst_ref=dst.at[i],
            send_sem=send_sem,
            recv_sem=recv_sem,
            device_id=(s, t),
            device_id_type=MESH,
        ).start()

    def keep(src, dst, recv_sem):
        pltpu.make_async_copy(src.at[SELF], dst.at[SELF], recv_sem).start()

    def got(src, dst, lo, hi, recv_sem):
        part = pl.ds(lo, hi - lo)
        pltpu.make_async_copy(src.at[part], dst.at[part], recv_sem).wait()

    loads[0].wait()
    loads[1].wait()
    loads[2].wait()
    lane = lax.broadcasted_iota(jnp.int32, (SLOTS, 128), 1)
    slot = lax.broadcasted_iota(jnp.int32, (SLOTS, 128), 0)
    lane_row = lax.broadcasted_iota(jnp.int32, (8, 128), 1)
    ids = jnp.zeros((8, 128), jnp.int32)
    for i, (s, t) in enumerate(others):
        ids = jnp.where(lane_row == i, s * 4 + t, ids)
    ids = jnp.concatenate([ids] * (SLOTS // 8), axis=0)
    name = jnp.zeros((SLOTS, 128), jnp.int32)
    rest_shift = jnp.zeros((SLOTS, 128), jnp.int32)
    place = jnp.zeros((SLOTS, 128), jnp.int32)
    early_slots = jnp.int32(0)
    for q in range(SLOTS):
        k = listed_ref[0, q]
        moved = shifts_ref[k]
        late = (moved >= 128).astype(jnp.int32)
        spot = early_slots + late * (2 * PAIRS - 1 - q)
        early_slots = early_slots + 1 - late
        name = jnp.where(slot == q, k, name)
        rest_shift = jnp.where(slot == q, moved - 128 * late, rest_shift)
        place = jnp.where(slot == q, spot, place)
    owner = name // OWN
    within = name - owner * OWN
    live = slot < counts_ref[0, 0]
    owned = owner == ids
    own_hot = owned.astype(jnp.bfloat16)
    asked = jnp.where(live, within + 1, 0).astype(jnp.bfloat16)
    name_out[:, 0, :] = lax.dot_general(own_hot, asked, TN, preferred_element_type=jnp.float32)

    pl.semaphore_wait(barrier, DEVICES - 1)
    for g in (0,):
        for i in range(*GROUPS[g]):
            if i < SELF:
                send(name_out, name_in, i, i, name_sems.at[3], name_sems.at[g])
    keep(name_out, name_in, name_sems.at[0])
    loads[5].wait()
    loads[3].wait()
    loads[4].wait()
    inv_mad[...] = jnp.broadcast_to((1.0 / mad_ref[...]).reshape(1, CHAN), (8, CHAN))
    for copy in loads[6:]:
        copy.wait()
    raw_v[:, 899:, :] = jnp.zeros((CHAN // 128, 5, 128), jnp.float32)
    chunks = CHAN // 128
    lane_block = lax.broadcasted_iota(jnp.int32, (ROWS, 128), 1)
    nothing = jnp.zeros((ROWS, 128), jnp.float32)

    def whiten_rows(start, base):
        across = [[], [], []]
        for k in range(chunks):
            taps = [raw_v[k, pl.ds(start + base + b, ROWS), :] for b in range(5)]
            for a in range(3):
                value = stencil_ref[a, 0] * taps[0]
                for b in range(1, 5):
                    value = value + stencil_ref[a, b] * taps[b]
                across[a].append(value)
        lower = [pltpu.roll(value, 1, 1) for value in across[0]]
        upper = [pltpu.roll(value, 127, 1) for value in across[2]]
        for k in range(chunks):
            left = jnp.where(lane_block == 0, lower[k - 1] if k else nothing, lower[k])
            right = jnp.where(
                lane_block == 127, upper[k + 1] if k < chunks - 1 else nothing, upper[k]
            )
            done = (across[1][k] + left + right) * inv_mad[0:1, 128 * k : 128 * k + 128]
            tile_v[pl.ds(base, ROWS), 128 * k : 128 * k + 128] = done

    def whiten(lo, hi):
        for t in range(lo, hi):

            def step(i, carry):
                for k in range(UNROLL):
                    whiten_rows(128 * t, pl.multiple_of((i * UNROLL + k) * ROWS, ROWS))
                return carry

            lax.fori_loop(0, 128 // ROWS // UNROLL, step, 0)
            here = slice(128 * t, 128 * t + 128)
            done = tile_v[:, :CHAN].T
            edge_v[0, :, here] = done[:16]
            edge_v[1, :, here] = done[CHAN - 16 :]
            done = done.astype(jnp.bfloat16)
            if t < TILES - 1:
                white[0, :, here] = done
            if t > 0:
                white[1, :, 128 * t - 128 : 128 * t] = done

    def halo(t):
        for side, k, a in ((0, chunks - 1, 0), (1, 0, 2)):
            value = stencil_ref[a, 0] * raw_v[k, 128 * t : 128 * t + 128, :]
            for b in range(1, 5):
                value = value + stencil_ref[a, b] * raw_v[k, 128 * t + b : 128 * t + b + 128, :]
            turned = value.T
            halo_out[side, :, 128 * t : 128 * t + 128] = turned[:8] if side else turned[120:]

    for t in range(TILES):
        halo(t)
    up = pltpu.make_async_remote_copy(
        src_ref=halo_out.at[0],
        dst_ref=halo_in.at[0],
        send_sem=halo_send.at[0],
        recv_sem=halo_recv.at[0],
        device_id=((sec + 1) % 32, tpl),
        device_id_type=MESH,
    )
    down = pltpu.make_async_remote_copy(
        src_ref=halo_out.at[1],
        dst_ref=halo_in.at[1],
        send_sem=halo_send.at[1],
        recv_sem=halo_recv.at[1],
        device_id=((sec + 31) % 32, tpl),
        device_id_type=MESH,
    )
    up.start()
    down.start()

    hot = place == lane
    index = jnp.sum(jnp.where(owned, lane, 0), axis=1, keepdims=True)
    info_v[0:1, :] = jnp.sum(jnp.where(hot, rest_shift, 0), axis=0, keepdims=True)
    info_v[1:2, :] = jnp.sum(jnp.where(hot, index, 0), axis=0, keepdims=True)
    info_v[2:8, :] = jnp.zeros((6, 128), jnp.int32)
    info = pltpu.make_async_copy(info_v, info_s, info_sem)
    info.start()
    even_hot = (place == 2 * lane).astype(jnp.bfloat16)
    odd_hot = (place == 2 * lane + 1).astype(jnp.bfloat16)
    even = lax.dot_general(even_hot, own_hot, TN, preferred_element_type=jnp.float32)[:32]
    odd = lax.dot_general(odd_hot, own_hot, TN, preferred_element_type=jnp.float32)[:32]
    pick_v[...] = jnp.concatenate([even] * 3 + [odd] * 3, axis=0).astype(jnp.bfloat16)
    acc[...] = jnp.zeros_like(acc)

    def answer(g):
        lo, hi = GROUPS[g]
        got(name_out, name_in, lo, hi, name_sems.at[g])
        wanted = name_in[lo:hi, 0, :]
        lanes = lax.broadcasted_iota(jnp.int32, (hi - lo, 128), 1)
        into = jnp.where(wanted == (lanes + 1).astype(jnp.float32), 1.0, 0.0).astype(jnp.bfloat16)
        chosen = jnp.dot(into[:, :OWN], templates_ref[...], preferred_element_type=jnp.float32)
        row_out[lo:hi] = chosen.reshape(hi - lo, 4, 128).astype(jnp.bfloat16)
        for i in range(lo, hi):
            if i < SELF:
                send(row_out, row_in, i, BACK[i], row_sems.at[0], row_sems.at[1])
        if hi == DEVICES:
            keep(row_out, row_in, row_sems.at[1])

    whiten(0, CUTS[0])
    answer(0)
    whiten(CUTS[0], TILES)

    lanes = lax.broadcasted_iota(jnp.int32, (DEVICES, 128), 1)
    into = jnp.where(name_in[:, 0, :] == (lanes + 1).astype(jnp.float32), 1.0, 0.0)
    into = into.astype(jnp.bfloat16)
    ones = jnp.ones((DEVICES, 128), jnp.bfloat16)
    tally = lax.dot_general(into, ones, TN, preferred_element_type=jnp.float32)
    tally_ref[...] = tally[:OWN]

    up.wait()
    down.wait()
    edge_row = lax.broadcasted_iota(jnp.int32, (16, WIDTH), 0)
    for side, row, end, channel, start in ((0, 7, 0, 0, 0), (1, 0, 31, CHAN - 1, CHAN - 16)):
        extra = halo_in[side, row : row + 1, :] * inv_mad[0:1, channel : channel + 1]
        hit = (edge_row == channel - start) & (sec != end)
        done = (edge_v[side] + jnp.where(hit, extra, 0.0)).astype(jnp.bfloat16)
        white[0, start : start + 16, :] = done[:, :WINDOW]
        white[1, start : start + 16, :] = done[:, 128:]

    info.wait()
    got(row_out, row_in, 0, DEVICES, row_sems.at[1])

    def prepare(j, band):
        for h in range(2):
            rows = row_in[info_s[1, 2 * j + h]].astype(jnp.float32)
            band[128 * h : 128 * h + 128, :] = build(rows, info_s[0, 2 * j + h])

    def correlate(j, band):
        half = (2 * j >= early_slots).astype(jnp.int32)
        corr = lax.dot_general(white[half], band[...], NT, preferred_element_type=jnp.float32)
        acc[j] = robust(corr).reshape(CHAN // 8, 8, 256).sum(axis=0)

    for u in range(LEAD):
        prepare(u, bands[u])
    for u in range(PAIRS):
        if u + LEAD < PAIRS:
            prepare(u + LEAD, bands[(u + LEAD) % NBANDS])
        correlate(u, bands[u % NBANDS])

    sums = jnp.sum(acc[...], axis=1)
    parts = jnp.concatenate(split3(sums[:, :128]) + split3(sums[:, 128:]), axis=0)
    part_out[:, 0, :] = lax.dot_general(pick_v[...], parts, TN, preferred_element_type=jnp.float32)
    for i in range(SELF):
        send(part_out, part_in, i, i, part_sems.at[0], part_sems.at[1])
    keep(part_out, part_in, part_sems.at[1])
    into = jnp.concatenate([into] * 3, axis=0)
    got(name_out, name_in, 0, SELF, name_sems.at[3])
    got(row_out, row_in, 0, SELF, row_sems.at[0])
    got(part_out, part_in, 0, DEVICES, part_sems.at[1])
    arrived = jnp.concatenate(split3(part_in[:, 0, :]), axis=0)
    total = lax.dot_general(into, arrived, TN, preferred_element_type=jnp.float32)
    total_ref[...] = total[:OWN]
    got(part_out, part_in, 0, SELF, part_sems.at[0])


def shards(raw, stencil, mad, templates, shifts, listed, counts):
    vmem = pl.BlockSpec(memory_space=pltpu.VMEM)
    hbm = pl.BlockSpec(memory_space=pl.ANY)
    f32 = jnp.float32
    dma = pltpu.SemaphoreType.DMA
    out = jax.ShapeDtypeStruct((OWN, LAGS), f32)
    total, tally = pl.pallas_call(
        kernel,
        out_shape=(out, out),
        in_specs=[hbm] * 7,
        out_specs=(vmem, vmem),
        scratch_shapes=[
            pltpu.VMEM((CHAN // 128, 904, 128), f32),
            pltpu.SMEM((3, 5), f32),
            pltpu.VMEM((CHAN,), f32),
            pltpu.VMEM((OWN, TLEN), jnp.bfloat16),
            pltpu.SMEM((2048,), jnp.int32),
            pltpu.SMEM((1, SLOTS), jnp.int32),
            pltpu.SMEM((1, 1), jnp.int32),
            pltpu.VMEM((128, CHAN), f32),
            pltpu.VMEM((2, 16, WIDTH), f32),
            pltpu.VMEM((2, 8, WIDTH), f32),
            pltpu.VMEM((2, 8, WIDTH), f32),
            pltpu.VMEM((2, CHAN, WINDOW), jnp.bfloat16),
            pltpu.VMEM((8, CHAN), f32),
            pltpu.VMEM((DEVICES, 1, 128), f32),
            pltpu.VMEM((DEVICES, 1, 128), f32),
            pltpu.VMEM((DEVICES, 4, 128), jnp.bfloat16),
            pltpu.VMEM((DEVICES, 4, 128), jnp.bfloat16),
            pltpu.VMEM((DEVICES, 1, 128), f32),
            pltpu.VMEM((DEVICES, 1, 128), f32),
            pltpu.VMEM((8, 128), jnp.int32),
            pltpu.SMEM((8, 128), jnp.int32),
            pltpu.VMEM((32, 8, 256), f32),
            pltpu.VMEM((6 * 32, 128), jnp.bfloat16),
        ]
        + [pltpu.VMEM((256, WINDOW), jnp.bfloat16)] * NBANDS
        + [dma((12,)), dma, dma((2,)), dma((2,)), dma((4,)), dma((2,)), dma((2,))],
        compiler_params=pltpu.CompilerParams(
            collective_id=0, has_side_effects=True, vmem_limit_bytes=60 * 2**20
        ),
        name="match",
    )(raw.T, stencil, mad, templates, shifts.reshape(-1), listed, counts)
    return total / jnp.sqrt(jnp.maximum(tally, 1.0) * CHAN)


def solution(mesh):
    in_specs = (
        P("sec", None),
        P(),
        P("sec"),
        P(("sec", "tpl"), None),
        P(None, "sec"),
        P("sec", "tpl"),
        P("sec", "tpl"),
    )
    out_specs = P(("sec", "tpl"), None)
    return jax.shard_map(shards, mesh=mesh, in_specs=in_specs, out_specs=out_specs, check_vma=False)
```

```python
import functools

import jax
import jax.numpy as jnp
from jax import lax
from jax.experimental import pallas as pl
from jax.experimental.pallas import tpu as pltpu
from jax.sharding import PartitionSpec as P

MESH = pl.DeviceIdType.MESH
DEVICES = 128
CHAN = 768
LAGS = 128
TLEN = 512
SLOTS = 32
OWN = 16
WINDOW = 768
WIDTH = 896
PAIRS = SLOTS // 2 + 1
NBANDS = 17
LEAD = 2
ROWS = 16
UNROLL = 4
TILES = WIDTH // 128
CUTS = (4,)
NT = (((1,), (1,)), ((), ()))
TN = (((0,), (0,)), ((), ()))


def hops(step):
    return sum((0, 1, 2, 1)[d] for d in step[:3])


STEPS = sorted(
    [
        (dz, dy, dx, dc)
        for dz in range(4)
        for dy in range(4)
        for dx in range(4)
        for dc in range(2)
    ],
    key=lambda step: (hops(step), step),
    reverse=True,
)
BACK = [
    STEPS.index(((4 - dz) % 4, (4 - dy) % 4, (4 - dx) % 4, dc)) for dz, dy, dx, dc in STEPS
]
SELF = DEVICES - 1
GROUPS = ((0, DEVICES),)


def peers():
    sec = lax.axis_index("sec")
    tpl = lax.axis_index("tpl")
    z = sec // 8
    y = sec // 2 % 4
    x = sec % 2 * 2 + tpl // 2
    core = tpl % 2
    zs = [(z + d) % 4 * 8 for d in range(4)]
    ys = [(y + d) % 4 * 2 for d in range(4)]
    xs = [(x + d) % 4 for d in range(4)]
    his = [v // 2 for v in xs]
    los = [v % 2 * 2 for v in xs]
    cores = [(core + d) % 2 for d in range(2)]
    out = []
    for dz, dy, dx, dc in STEPS:
        s = zs[dz] + ys[dy] + his[dx]
        t = los[dx] + cores[dc]
        out.append((s, t))
    return sec, tpl, out


def robust(value):
    return value * lax.rsqrt(1.0 + value * value)


def build(band, at, rows, shift):
    flat = jnp.concatenate(
        [jnp.broadcast_to(rows[k : k + 1], (8, 128)) for k in range(4)]
        + [jnp.zeros((8, WINDOW - TLEN), jnp.float32)],
        axis=1,
    )
    base = pltpu.roll(flat, shift, 1)
    base = pltpu.roll(base, 0, 1, stride=1, stride_axis=0)
    for g in range(8):
        pair = [pltpu.roll(base, 8 * k, 1) if k else base for k in (2 * g, 2 * g + 1)]
        band[at + 16 * g : at + 16 * g + 16, :] = jnp.concatenate(pair, axis=0).astype(jnp.bfloat16)


def split3(value):
    high = value.astype(jnp.bfloat16)
    left = value - high.astype(jnp.float32)
    middle = left.astype(jnp.bfloat16)
    low = (left - middle.astype(jnp.float32)).astype(jnp.bfloat16)
    return [high, middle, low]


def kernel(
    raw_hbm,
    stencil_hbm,
    mad_hbm,
    templates_hbm,
    shifts_hbm,
    listed_hbm,
    counts_hbm,
    total_ref,
    tally_ref,
    raw_v,
    stencil_ref,
    mad_ref,
    templates_ref,
    shifts_ref,
    listed_ref,
    counts_ref,
    tile_v,
    edge_v,
    halo_out,
    halo_in,
    white,
    inv_mad,
    name_out,
    name_in,
    row_out,
    row_in,
    part_out,
    part_in,
    info_v,
    info_s,
    acc,
    pick_v,
    *rest,
):
    bands = rest[:NBANDS]
    load_sems, info_sem, halo_send, halo_recv, name_sems, row_sems, part_sems = rest[NBANDS:]
    sec, tpl, others = peers()

    barrier = pltpu.get_barrier_semaphore()
    loads = [
        pltpu.make_async_copy(src, dst, load_sems.at[k])
        for k, (src, dst) in enumerate(
            [
                (listed_hbm, listed_ref),
                (counts_hbm, counts_ref),
                (shifts_hbm, shifts_ref),
                (stencil_hbm, stencil_ref),
                (mad_hbm, mad_ref),
                (templates_hbm, templates_ref),
            ]
            + [(raw_hbm.at[:, pl.ds(128 * k, 128)], raw_v.at[k, pl.ds(0, 899)]) for k in range(CHAN // 128)]
        )
    ]
    for copy in loads[:3]:
        copy.start()
    for s, t in others[:SELF]:
        pl.semaphore_signal(barrier, inc=1, device_id=(s, t), device_id_type=MESH)
    for copy in loads[3:]:
        copy.start()

    def send(src, dst, i, to, send_sem, recv_sem):
        s, t = others[to]
        pltpu.make_async_remote_copy(
            src_ref=src.at[i],
            dst_ref=dst.at[i],
            send_sem=send_sem,
            recv_sem=recv_sem,
            device_id=(s, t),
            device_id_type=MESH,
        ).start()

    def keep(src, dst, recv_sem):
        pltpu.make_async_copy(src.at[SELF], dst.at[SELF], recv_sem).start()

    def got(src, dst, lo, hi, recv_sem):
        part = pl.ds(lo, hi - lo)
        pltpu.make_async_copy(src.at[part], dst.at[part], recv_sem).wait()

    loads[0].wait()
    loads[1].wait()
    loads[2].wait()
    lane = lax.broadcasted_iota(jnp.int32, (SLOTS, 128), 1)
    slot = lax.broadcasted_iota(jnp.int32, (SLOTS, 128), 0)
    lane_row = lax.broadcasted_iota(jnp.int32, (8, 128), 1)
    ids = jnp.zeros((8, 128), jnp.int32)
    for i, (s, t) in enumerate(others):
        ids = jnp.where(lane_row == i, s * 4 + t, ids)
    ids = jnp.concatenate([ids] * (SLOTS // 8), axis=0)
    name = jnp.zeros((SLOTS, 128), jnp.int32)
    rest_shift = jnp.zeros((SLOTS, 128), jnp.int32)
    place = jnp.zeros((SLOTS, 128), jnp.int32)
    early_slots = jnp.int32(0)
    for q in range(SLOTS):
        k = listed_ref[0, q]
        moved = shifts_ref[k]
        late = (moved >= 128).astype(jnp.int32)
        spot = early_slots + late * (2 * PAIRS - 1 - q)
        early_slots = early_slots + 1 - late
        name = jnp.where(slot == q, k, name)
        rest_shift = jnp.where(slot == q, moved - 128 * late, rest_shift)
        place = jnp.where(slot == q, spot, place)
    owner = name // OWN
    within = name - owner * OWN
    live = slot < counts_ref[0, 0]
    owned = owner == ids
    own_hot = owned.astype(jnp.bfloat16)
    asked = jnp.where(live, within + 1, 0).astype(jnp.bfloat16)
    name_out[:, 0, :] = lax.dot_general(own_hot, asked, TN, preferred_element_type=jnp.float32)

    pl.semaphore_wait(barrier, DEVICES - 1)
    for g in (0,):
        for i in range(*GROUPS[g]):
            if i < SELF:
                send(name_out, name_in, i, i, name_sems.at[3], name_sems.at[g])
    keep(name_out, name_in, name_sems.at[0])
    loads[5].wait()
    loads[3].wait()
    loads[4].wait()
    inv_mad[...] = jnp.broadcast_to((1.0 / mad_ref[...]).reshape(1, CHAN), (8, CHAN))
    for copy in loads[6:]:
        copy.wait()
    raw_v[:, 899:, :] = jnp.zeros((CHAN // 128, 5, 128), jnp.float32)
    chunks = CHAN // 128
    lane_block = lax.broadcasted_iota(jnp.int32, (ROWS, 128), 1)
    nothing = jnp.zeros((ROWS, 128), jnp.float32)

    def whiten_rows(start, base):
        across = [[], [], []]
        for k in range(chunks):
            taps = [raw_v[k, pl.ds(start + base + b, ROWS), :] for b in range(5)]
            for a in range(3):
                value = stencil_ref[a, 0] * taps[0]
                for b in range(1, 5):
                    value = value + stencil_ref[a, b] * taps[b]
                across[a].append(value)
        lower = [pltpu.roll(value, 1, 1) for value in across[0]]
        upper = [pltpu.roll(value, 127, 1) for value in across[2]]
        for k in range(chunks):
            left = jnp.where(lane_block == 0, lower[k - 1] if k else nothing, lower[k])
            right = jnp.where(
                lane_block == 127, upper[k + 1] if k < chunks - 1 else nothing, upper[k]
            )
            done = (across[1][k] + left + right) * inv_mad[0:1, 128 * k : 128 * k + 128]
            tile_v[pl.ds(base, ROWS), 128 * k : 128 * k + 128] = done

    def whiten(lo, hi):
        for t in range(lo, hi):

            def step(i, carry):
                for k in range(UNROLL):
                    whiten_rows(128 * t, pl.multiple_of((i * UNROLL + k) * ROWS, ROWS))
                return carry

            lax.fori_loop(0, 128 // ROWS // UNROLL, step, 0)
            here = slice(128 * t, 128 * t + 128)
            done = tile_v[:, :CHAN].T
            edge_v[0, :, here] = done[:16]
            edge_v[1, :, here] = done[CHAN - 16 :]
            done = done.astype(jnp.bfloat16)
            if t < TILES - 1:
                white[0, :, here] = done
            if t > 0:
                white[1, :, 128 * t - 128 : 128 * t] = done

    def halo(t):
        for side, k, a in ((0, chunks - 1, 0), (1, 0, 2)):
            value = stencil_ref[a, 0] * raw_v[k, 128 * t : 128 * t + 128, :]
            for b in range(1, 5):
                value = value + stencil_ref[a, b] * raw_v[k, 128 * t + b : 128 * t + b + 128, :]
            turned = value.T
            halo_out[side, :, 128 * t : 128 * t + 128] = turned[:8] if side else turned[120:]

    for t in range(TILES):
        halo(t)
    up = pltpu.make_async_remote_copy(
        src_ref=halo_out.at[0],
        dst_ref=halo_in.at[0],
        send_sem=halo_send.at[0],
        recv_sem=halo_recv.at[0],
        device_id=((sec + 1) % 32, tpl),
        device_id_type=MESH,
    )
    down = pltpu.make_async_remote_copy(
        src_ref=halo_out.at[1],
        dst_ref=halo_in.at[1],
        send_sem=halo_send.at[1],
        recv_sem=halo_recv.at[1],
        device_id=((sec + 31) % 32, tpl),
        device_id_type=MESH,
    )
    up.start()
    down.start()

    hot = place == lane
    index = jnp.sum(jnp.where(owned, lane, 0), axis=1, keepdims=True)
    info_v[0:1, :] = jnp.sum(jnp.where(hot, rest_shift, 0), axis=0, keepdims=True)
    info_v[1:2, :] = jnp.sum(jnp.where(hot, index, 0), axis=0, keepdims=True)
    info_v[2:8, :] = jnp.zeros((6, 128), jnp.int32)
    info = pltpu.make_async_copy(info_v, info_s, info_sem)
    info.start()
    even_hot = (place == 2 * lane).astype(jnp.bfloat16)
    odd_hot = (place == 2 * lane + 1).astype(jnp.bfloat16)
    even = lax.dot_general(even_hot, own_hot, TN, preferred_element_type=jnp.float32)[:32]
    odd = lax.dot_general(odd_hot, own_hot, TN, preferred_element_type=jnp.float32)[:32]
    pick_v[...] = jnp.concatenate([even] * 3 + [odd] * 3, axis=0).astype(jnp.bfloat16)
    acc[...] = jnp.zeros_like(acc)

    def answer(g):
        lo, hi = GROUPS[g]
        got(name_out, name_in, lo, hi, name_sems.at[g])
        wanted = name_in[lo:hi, 0, :]
        lanes = lax.broadcasted_iota(jnp.int32, (hi - lo, 128), 1)
        into = jnp.where(wanted == (lanes + 1).astype(jnp.float32), 1.0, 0.0).astype(jnp.bfloat16)
        chosen = jnp.dot(into[:, :OWN], templates_ref[...], preferred_element_type=jnp.float32)
        row_out[lo:hi] = chosen.reshape(hi - lo, 4, 128).astype(jnp.bfloat16)
        for i in range(lo, hi):
            if i < SELF:
                send(row_out, row_in, i, BACK[i], row_sems.at[0], row_sems.at[1])
        if hi == DEVICES:
            keep(row_out, row_in, row_sems.at[1])

    whiten(0, CUTS[0])
    answer(0)
    whiten(CUTS[0], TILES)

    lanes = lax.broadcasted_iota(jnp.int32, (DEVICES, 128), 1)
    into = jnp.where(name_in[:, 0, :] == (lanes + 1).astype(jnp.float32), 1.0, 0.0)
    into = into.astype(jnp.bfloat16)
    ones = jnp.ones((DEVICES, 128), jnp.bfloat16)
    tally = lax.dot_general(into, ones, TN, preferred_element_type=jnp.float32)
    tally_ref[...] = tally[:OWN]

    up.wait()
    down.wait()
    edge_row = lax.broadcasted_iota(jnp.int32, (16, WIDTH), 0)
    for side, row, end, channel, start in ((0, 7, 0, 0, 0), (1, 0, 31, CHAN - 1, CHAN - 16)):
        extra = halo_in[side, row : row + 1, :] * inv_mad[0:1, channel : channel + 1]
        hit = (edge_row == channel - start) & (sec != end)
        done = (edge_v[side] + jnp.where(hit, extra, 0.0)).astype(jnp.bfloat16)
        white[0, start : start + 16, :] = done[:, :WINDOW]
        white[1, start : start + 16, :] = done[:, 128:]

    info.wait()
    got(row_out, row_in, 0, DEVICES, row_sems.at[1])

    def prepare(j, band):
        for h in range(2):
            rows = row_in[info_s[1, 2 * j + h]].astype(jnp.float32)
            build(band, 128 * h, rows, info_s[0, 2 * j + h])

    def correlate(j, band):
        half = (2 * j >= early_slots).astype(jnp.int32)
        corr = lax.dot_general(white[half], band[...], NT, preferred_element_type=jnp.float32)
        acc[j] = robust(corr).reshape(CHAN // 8, 8, 256).sum(axis=0)

    for u in range(LEAD):
        prepare(u, bands[u])
    for u in range(PAIRS):
        if u + LEAD < PAIRS:
            prepare(u + LEAD, bands[(u + LEAD) % NBANDS])
        correlate(u, bands[u % NBANDS])

    sums = jnp.sum(acc[...], axis=1)
    parts = jnp.concatenate(split3(sums[:, :128]) + split3(sums[:, 128:]), axis=0)
    part_out[:, 0, :] = lax.dot_general(pick_v[...], parts, TN, preferred_element_type=jnp.float32)
    for i in range(SELF):
        send(part_out, part_in, i, i, part_sems.at[0], part_sems.at[1])
    keep(part_out, part_in, part_sems.at[1])
    into = jnp.concatenate([into] * 3, axis=0)
    got(name_out, name_in, 0, SELF, name_sems.at[3])
    got(row_out, row_in, 0, SELF, row_sems.at[0])
    got(part_out, part_in, 0, DEVICES, part_sems.at[1])
    arrived = jnp.concatenate(split3(part_in[:, 0, :]), axis=0)
    total = lax.dot_general(into, arrived, TN, preferred_element_type=jnp.float32)
    total_ref[...] = total[:OWN]
    got(part_out, part_in, 0, SELF, part_sems.at[0])


def shards(raw, stencil, mad, templates, shifts, listed, counts):
    vmem = pl.BlockSpec(memory_space=pltpu.VMEM)
    hbm = pl.BlockSpec(memory_space=pl.ANY)
    f32 = jnp.float32
    dma = pltpu.SemaphoreType.DMA
    out = jax.ShapeDtypeStruct((OWN, LAGS), f32)
    total, tally = pl.pallas_call(
        kernel,
        out_shape=(out, out),
        in_specs=[hbm] * 7,
        out_specs=(vmem, vmem),
        scratch_shapes=[
            pltpu.VMEM((CHAN // 128, 904, 128), f32),
            pltpu.SMEM((3, 5), f32),
            pltpu.VMEM((CHAN,), f32),
            pltpu.VMEM((OWN, TLEN), jnp.bfloat16),
            pltpu.SMEM((2048,), jnp.int32),
            pltpu.SMEM((1, SLOTS), jnp.int32),
            pltpu.SMEM((1, 1), jnp.int32),
            pltpu.VMEM((128, CHAN), f32),
            pltpu.VMEM((2, 16, WIDTH), f32),
            pltpu.VMEM((2, 8, WIDTH), f32),
            pltpu.VMEM((2, 8, WIDTH), f32),
            pltpu.VMEM((2, CHAN, WINDOW), jnp.bfloat16),
            pltpu.VMEM((8, CHAN), f32),
            pltpu.VMEM((DEVICES, 1, 128), f32),
            pltpu.VMEM((DEVICES, 1, 128), f32),
            pltpu.VMEM((DEVICES, 4, 128), jnp.bfloat16),
            pltpu.VMEM((DEVICES, 4, 128), jnp.bfloat16),
            pltpu.VMEM((DEVICES, 1, 128), f32),
            pltpu.VMEM((DEVICES, 1, 128), f32),
            pltpu.VMEM((8, 128), jnp.int32),
            pltpu.SMEM((8, 128), jnp.int32),
            pltpu.VMEM((32, 8, 256), f32),
            pltpu.VMEM((6 * 32, 128), jnp.bfloat16),
        ]
        + [pltpu.VMEM((256, WINDOW), jnp.bfloat16)] * NBANDS
        + [dma((12,)), dma, dma((2,)), dma((2,)), dma((4,)), dma((2,)), dma((2,))],
        compiler_params=pltpu.CompilerParams(
            collective_id=0, has_side_effects=True, vmem_limit_bytes=60 * 2**20
        ),
        name="match",
    )(raw.T, stencil, mad, templates, shifts.reshape(-1), listed, counts)
    return total / jnp.sqrt(jnp.maximum(tally, 1.0) * CHAN)


def solution(mesh):
    in_specs = (
        P("sec", None),
        P(),
        P("sec"),
        P(("sec", "tpl"), None),
        P(None, "sec"),
        P("sec", "tpl"),
        P("sec", "tpl"),
    )
    out_specs = P(("sec", "tpl"), None)
    return jax.shard_map(shards, mesh=mesh, in_specs=in_specs, out_specs=out_specs, check_vma=False)
```

```python
import functools

import jax
import jax.numpy as jnp
from jax import lax
from jax.experimental import pallas as pl
from jax.experimental.pallas import tpu as pltpu
from jax.sharding import PartitionSpec as P

MESH = pl.DeviceIdType.MESH
DEVICES = 128
CHAN = 768
LAGS = 128
TLEN = 512
SLOTS = 32
OWN = 16
WINDOW = 768
WIDTH = 896
PAIRS = SLOTS // 2 + 1
NBANDS = 17
LEAD = 2
ROWS = 16
UNROLL = 4
TILES = WIDTH // 128
CUTS = (4,)
NT = (((1,), (1,)), ((), ()))
TN = (((0,), (0,)), ((), ()))


def hops(step):
    return sum((0, 1, 2, 1)[d] for d in step[:3])


STEPS = sorted(
    [
        (dz, dy, dx, dc)
        for dz in range(4)
        for dy in range(4)
        for dx in range(4)
        for dc in range(2)
    ],
    key=lambda step: (hops(step), step),
    reverse=True,
)
BACK = [
    STEPS.index(((4 - dz) % 4, (4 - dy) % 4, (4 - dx) % 4, dc)) for dz, dy, dx, dc in STEPS
]
SELF = DEVICES - 1
GROUPS = ((0, DEVICES),)


def peers():
    sec = lax.axis_index("sec")
    tpl = lax.axis_index("tpl")
    z = sec // 8
    y = sec // 2 % 4
    x = sec % 2 * 2 + tpl // 2
    core = tpl % 2
    zs = [(z + d) % 4 * 8 for d in range(4)]
    ys = [(y + d) % 4 * 2 for d in range(4)]
    xs = [(x + d) % 4 for d in range(4)]
    his = [v // 2 for v in xs]
    los = [v % 2 * 2 for v in xs]
    cores = [(core + d) % 2 for d in range(2)]
    out = []
    for dz, dy, dx, dc in STEPS:
        s = zs[dz] + ys[dy] + his[dx]
        t = los[dx] + cores[dc]
        out.append((s, t))
    return sec, tpl, out


def robust(value):
    return value * lax.rsqrt(1.0 + value * value)


def build(band, at, rows, shift):
    flat = jnp.concatenate(
        [jnp.broadcast_to(rows[k : k + 1], (8, 128)) for k in range(4)]
        + [jnp.zeros((8, WINDOW - TLEN), jnp.float32)],
        axis=1,
    )
    base = pltpu.roll(flat, shift, 1)
    base = pltpu.roll(base, 0, 1, stride=1, stride_axis=0)
    for g in range(8):
        pair = [pltpu.roll(base, 8 * k, 1) if k else base for k in (2 * g, 2 * g + 1)]
        band[at + 16 * g : at + 16 * g + 16, :] = jnp.concatenate(pair, axis=0).astype(jnp.bfloat16)


def split3(value):
    high = value.astype(jnp.bfloat16)
    left = value - high.astype(jnp.float32)
    middle = left.astype(jnp.bfloat16)
    low = (left - middle.astype(jnp.float32)).astype(jnp.bfloat16)
    return [high, middle, low]


def kernel(
    raw_hbm,
    stencil_hbm,
    mad_hbm,
    templates_hbm,
    shifts_hbm,
    listed_hbm,
    counts_hbm,
    total_ref,
    tally_ref,
    raw_v,
    stencil_ref,
    mad_ref,
    templates_ref,
    shifts_ref,
    listed_ref,
    counts_ref,
    tile_v,
    edge_v,
    halo_out,
    halo_in,
    white,
    inv_mad,
    name_out,
    name_in,
    row_out,
    row_in,
    part_out,
    part_in,
    info_v,
    info_s,
    acc,
    pick_v,
    *rest,
):
    bands = rest[:NBANDS]
    load_sems, info_sem, halo_send, halo_recv, name_sems, row_sems, part_sems = rest[NBANDS:]
    sec, tpl, others = peers()

    barrier = pltpu.get_barrier_semaphore()
    loads = [
        pltpu.make_async_copy(src, dst, load_sems.at[k])
        for k, (src, dst) in enumerate(
            [
                (listed_hbm, listed_ref),
                (counts_hbm, counts_ref),
                (shifts_hbm, shifts_ref),
                (stencil_hbm, stencil_ref),
                (mad_hbm, mad_ref),
                (templates_hbm, templates_ref),
            ]
            + [(raw_hbm.at[:, pl.ds(128 * k, 128)], raw_v.at[k, pl.ds(0, 899)]) for k in range(CHAN // 128)]
        )
    ]
    for copy in loads[:3]:
        copy.start()
    for s, t in others[:SELF]:
        pl.semaphore_signal(barrier, inc=1, device_id=(s, t), device_id_type=MESH)
    for copy in loads[3:]:
        copy.start()

    def send(src, dst, i, to, send_sem, recv_sem):
        s, t = others[to]
        pltpu.make_async_remote_copy(
            src_ref=src.at[i],
            dst_ref=dst.at[i],
            send_sem=send_sem,
            recv_sem=recv_sem,
            device_id=(s, t),
            device_id_type=MESH,
        ).start()

    def keep(src, dst, recv_sem):
        pltpu.make_async_copy(src.at[SELF], dst.at[SELF], recv_sem).start()

    def got(src, dst, lo, hi, recv_sem):
        part = pl.ds(lo, hi - lo)
        pltpu.make_async_copy(src.at[part], dst.at[part], recv_sem).wait()

    loads[0].wait()
    loads[1].wait()
    loads[2].wait()
    lane = lax.broadcasted_iota(jnp.int32, (SLOTS, 128), 1)
    slot = lax.broadcasted_iota(jnp.int32, (SLOTS, 128), 0)
    lane_row = lax.broadcasted_iota(jnp.int32, (8, 128), 1)
    ids = jnp.zeros((8, 128), jnp.int32)
    for i, (s, t) in enumerate(others):
        ids = jnp.where(lane_row == i, s * 4 + t, ids)
    ids = jnp.concatenate([ids] * (SLOTS // 8), axis=0)
    name = jnp.zeros((SLOTS, 128), jnp.int32)
    rest_shift = jnp.zeros((SLOTS, 128), jnp.int32)
    place = jnp.zeros((SLOTS, 128), jnp.int32)
    early_slots = jnp.int32(0)
    for q in range(SLOTS):
        k = listed_ref[0, q]
        moved = shifts_ref[k]
        late = (moved >= 128).astype(jnp.int32)
        spot = early_slots + late * (2 * PAIRS - 1 - q)
        early_slots = early_slots + 1 - late
        name = jnp.where(slot == q, k, name)
        rest_shift = jnp.where(slot == q, moved - 128 * late, rest_shift)
        place = jnp.where(slot == q, spot, place)
    owner = name // OWN
    within = name - owner * OWN
    live = slot < counts_ref[0, 0]
    owned = owner == ids
    own_hot = owned.astype(jnp.bfloat16)
    asked = jnp.where(live, within + 1, 0).astype(jnp.bfloat16)
    name_out[:, 0, :] = lax.dot_general(own_hot, asked, TN, preferred_element_type=jnp.float32)

    pl.semaphore_wait(barrier, DEVICES - 1)
    for g in (0,):
        for i in range(*GROUPS[g]):
            if i < SELF:
                send(name_out, name_in, i, i, name_sems.at[3], name_sems.at[g])
    keep(name_out, name_in, name_sems.at[0])
    loads[5].wait()
    loads[3].wait()
    loads[4].wait()
    inv_mad[...] = jnp.broadcast_to((1.0 / mad_ref[...]).reshape(1, CHAN), (8, CHAN))
    for copy in loads[6:]:
        copy.wait()
    raw_v[:, 899:, :] = jnp.zeros((CHAN // 128, 5, 128), jnp.float32)
    chunks = CHAN // 128
    lane_block = lax.broadcasted_iota(jnp.int32, (ROWS, 128), 1)
    nothing = jnp.zeros((ROWS, 128), jnp.float32)

    def whiten_rows(start, base):
        across = [[], [], []]
        for k in range(chunks):
            taps = [raw_v[k, pl.ds(start + base + b, ROWS), :] for b in range(5)]
            for a in range(3):
                value = stencil_ref[a, 0] * taps[0]
                for b in range(1, 5):
                    value = value + stencil_ref[a, b] * taps[b]
                across[a].append(value)
        lower = [pltpu.roll(value, 1, 1) for value in across[0]]
        upper = [pltpu.roll(value, 127, 1) for value in across[2]]
        for k in range(chunks):
            left = jnp.where(lane_block == 0, lower[k - 1] if k else nothing, lower[k])
            right = jnp.where(
                lane_block == 127, upper[k + 1] if k < chunks - 1 else nothing, upper[k]
            )
            done = (across[1][k] + left + right) * inv_mad[0:1, 128 * k : 128 * k + 128]
            tile_v[pl.ds(base, ROWS), 128 * k : 128 * k + 128] = done

    def whiten(lo, hi):
        for t in range(lo, hi):

            def step(i, carry):
                for k in range(UNROLL):
                    whiten_rows(128 * t, pl.multiple_of((i * UNROLL + k) * ROWS, ROWS))
                return carry

            lax.fori_loop(0, 128 // ROWS // UNROLL, step, 0)
            here = slice(128 * t, 128 * t + 128)
            done = tile_v[:, :CHAN].T
            edge_v[0, :, here] = done[:16]
            edge_v[1, :, here] = done[CHAN - 16 :]
            done = done.astype(jnp.bfloat16)
            if t < TILES - 1:
                white[0, :, here] = done
            if t > 0:
                white[1, :, 128 * t - 128 : 128 * t] = done

    def halo(t):
        for side, k, a in ((0, chunks - 1, 0), (1, 0, 2)):
            value = stencil_ref[a, 0] * raw_v[k, 128 * t : 128 * t + 128, :]
            for b in range(1, 5):
                value = value + stencil_ref[a, b] * raw_v[k, 128 * t + b : 128 * t + b + 128, :]
            turned = value.T
            halo_out[side, :, 128 * t : 128 * t + 128] = turned[:8] if side else turned[120:]

    for t in range(TILES):
        halo(t)
    up = pltpu.make_async_remote_copy(
        src_ref=halo_out.at[0],
        dst_ref=halo_in.at[0],
        send_sem=halo_send.at[0],
        recv_sem=halo_recv.at[0],
        device_id=((sec + 1) % 32, tpl),
        device_id_type=MESH,
    )
    down = pltpu.make_async_remote_copy(
        src_ref=halo_out.at[1],
        dst_ref=halo_in.at[1],
        send_sem=halo_send.at[1],
        recv_sem=halo_recv.at[1],
        device_id=((sec + 31) % 32, tpl),
        device_id_type=MESH,
    )
    up.start()
    down.start()

    hot = place == lane
    index = jnp.sum(jnp.where(owned, lane, 0), axis=1, keepdims=True)
    info_v[0:1, :] = jnp.sum(jnp.where(hot, rest_shift, 0), axis=0, keepdims=True)
    info_v[1:2, :] = jnp.sum(jnp.where(hot, index, 0), axis=0, keepdims=True)
    info_v[2:8, :] = jnp.zeros((6, 128), jnp.int32)
    info = pltpu.make_async_copy(info_v, info_s, info_sem)
    info.start()
    even_hot = (place == 2 * lane).astype(jnp.bfloat16)
    odd_hot = (place == 2 * lane + 1).astype(jnp.bfloat16)
    even = lax.dot_general(even_hot, own_hot, TN, preferred_element_type=jnp.float32)[:32]
    odd = lax.dot_general(odd_hot, own_hot, TN, preferred_element_type=jnp.float32)[:32]
    pick_v[...] = jnp.concatenate([even] * 3 + [odd] * 3, axis=0).T.astype(jnp.bfloat16)
    acc[...] = jnp.zeros_like(acc)

    def answer(g):
        lo, hi = GROUPS[g]
        got(name_out, name_in, lo, hi, name_sems.at[g])
        wanted = name_in[lo:hi, 0, :]
        lanes = lax.broadcasted_iota(jnp.int32, (hi - lo, 128), 1)
        into = jnp.where(wanted == (lanes + 1).astype(jnp.float32), 1.0, 0.0).astype(jnp.bfloat16)
        chosen = jnp.dot(into[:, :OWN], templates_ref[...], preferred_element_type=jnp.float32)
        row_out[lo:hi] = chosen.reshape(hi - lo, 4, 128).astype(jnp.bfloat16)
        for i in range(lo, hi):
            if i < SELF:
                send(row_out, row_in, i, BACK[i], row_sems.at[0], row_sems.at[1])
        if hi == DEVICES:
            keep(row_out, row_in, row_sems.at[1])

    whiten(0, CUTS[0])
    answer(0)
    whiten(CUTS[0], TILES)

    lanes = lax.broadcasted_iota(jnp.int32, (DEVICES, 128), 1)
    into = jnp.where(name_in[:, 0, :] == (lanes + 1).astype(jnp.float32), 1.0, 0.0)
    turned = jnp.concatenate([into.T[:OWN]] * 3, axis=1).astype(jnp.bfloat16)
    into = into.astype(jnp.bfloat16)
    ones = jnp.ones((DEVICES, 128), jnp.bfloat16)
    tally = lax.dot_general(into, ones, TN, preferred_element_type=jnp.float32)
    tally_ref[...] = tally[:OWN]

    up.wait()
    down.wait()
    edge_row = lax.broadcasted_iota(jnp.int32, (16, WIDTH), 0)
    for side, row, end, channel, start in ((0, 7, 0, 0, 0), (1, 0, 31, CHAN - 1, CHAN - 16)):
        extra = halo_in[side, row : row + 1, :] * inv_mad[0:1, channel : channel + 1]
        hit = (edge_row == channel - start) & (sec != end)
        done = (edge_v[side] + jnp.where(hit, extra, 0.0)).astype(jnp.bfloat16)
        white[0, start : start + 16, :] = done[:, :WINDOW]
        white[1, start : start + 16, :] = done[:, 128:]

    info.wait()
    got(row_out, row_in, 0, DEVICES, row_sems.at[1])

    def prepare(j, band):
        for h in range(2):
            rows = row_in[info_s[1, 2 * j + h]].astype(jnp.float32)
            build(band, 128 * h, rows, info_s[0, 2 * j + h])

    def correlate(j, band):
        half = (2 * j >= early_slots).astype(jnp.int32)
        corr = lax.dot_general(white[half], band[...], NT, preferred_element_type=jnp.float32)
        acc[j] = robust(corr).reshape(CHAN // 8, 8, 256).sum(axis=0)

    for u in range(LEAD):
        prepare(u, bands[u])
    for u in range(PAIRS):
        if u + LEAD < PAIRS:
            prepare(u + LEAD, bands[(u + LEAD) % NBANDS])
        correlate(u, bands[u % NBANDS])

    sums = jnp.sum(acc[...], axis=1)
    parts = jnp.concatenate(split3(sums[:, :128]) + split3(sums[:, 128:]), axis=0)
    part_out[:, 0, :] = jnp.dot(pick_v[...], parts, preferred_element_type=jnp.float32)
    for i in range(SELF):
        send(part_out, part_in, i, i, part_sems.at[0], part_sems.at[1])
    keep(part_out, part_in, part_sems.at[1])
    got(name_out, name_in, 0, SELF, name_sems.at[3])
    got(row_out, row_in, 0, SELF, row_sems.at[0])
    got(part_out, part_in, 0, DEVICES, part_sems.at[1])
    arrived = jnp.concatenate(split3(part_in[:, 0, :]), axis=0)
    total = jnp.dot(turned, arrived, preferred_element_type=jnp.float32)
    total_ref[...] = total
    got(part_out, part_in, 0, SELF, part_sems.at[0])


def shards(raw, stencil, mad, templates, shifts, listed, counts):
    vmem = pl.BlockSpec(memory_space=pltpu.VMEM)
    hbm = pl.BlockSpec(memory_space=pl.ANY)
    f32 = jnp.float32
    dma = pltpu.SemaphoreType.DMA
    out = jax.ShapeDtypeStruct((OWN, LAGS), f32)
    total, tally = pl.pallas_call(
        kernel,
        out_shape=(out, out),
        in_specs=[hbm] * 7,
        out_specs=(vmem, vmem),
        scratch_shapes=[
            pltpu.VMEM((CHAN // 128, 904, 128), f32),
            pltpu.SMEM((3, 5), f32),
            pltpu.VMEM((CHAN,), f32),
            pltpu.VMEM((OWN, TLEN), jnp.bfloat16),
            pltpu.SMEM((2048,), jnp.int32),
            pltpu.SMEM((1, SLOTS), jnp.int32),
            pltpu.SMEM((1, 1), jnp.int32),
            pltpu.VMEM((128, CHAN), f32),
            pltpu.VMEM((2, 16, WIDTH), f32),
            pltpu.VMEM((2, 8, WIDTH), f32),
            pltpu.VMEM((2, 8, WIDTH), f32),
            pltpu.VMEM((2, CHAN, WINDOW), jnp.bfloat16),
            pltpu.VMEM((8, CHAN), f32),
            pltpu.VMEM((DEVICES, 1, 128), f32),
            pltpu.VMEM((DEVICES, 1, 128), f32),
            pltpu.VMEM((DEVICES, 4, 128), jnp.bfloat16),
            pltpu.VMEM((DEVICES, 4, 128), jnp.bfloat16),
            pltpu.VMEM((DEVICES, 1, 128), f32),
            pltpu.VMEM((DEVICES, 1, 128), f32),
            pltpu.VMEM((8, 128), jnp.int32),
            pltpu.SMEM((8, 128), jnp.int32),
            pltpu.VMEM((32, 8, 256), f32),
            pltpu.VMEM((128, 6 * 32), jnp.bfloat16),
        ]
        + [pltpu.VMEM((256, WINDOW), jnp.bfloat16)] * NBANDS
        + [dma((12,)), dma, dma((2,)), dma((2,)), dma((4,)), dma((2,)), dma((2,))],
        compiler_params=pltpu.CompilerParams(
            collective_id=0, has_side_effects=True, vmem_limit_bytes=60 * 2**20
        ),
        name="match",
    )(raw.T, stencil, mad, templates, shifts.reshape(-1), listed, counts)
    return total / jnp.sqrt(jnp.maximum(tally, 1.0) * CHAN)


def solution(mesh):
    in_specs = (
        P("sec", None),
        P(),
        P("sec"),
        P(("sec", "tpl"), None),
        P(None, "sec"),
        P("sec", "tpl"),
        P("sec", "tpl"),
    )
    out_specs = P(("sec", "tpl"), None)
    return jax.shard_map(shards, mesh=mesh, in_specs=in_specs, out_specs=out_specs, check_vma=False)
```
